256 devices in a mesh: member: 8 (over x, core), region: 32 (over z, y).
Axes of the slice: x: 4, y: 4, z: 8, core: 2. Of those that a mesh axis runs over, the one named last changes fastest.
Arguments:
- background: bfloat16 [128, 4096, 512], P('member', 'region'), may hold values from -6 to 6
- obs_anom: bfloat16 [128, 131072], P('member', 'region'), may hold values from -6 to 6
- innovation: float32 [131072], P('region'), may hold values from -6 to 6
- obs_error: float32 [131072], P('region'), may hold values from 0.5 to 2
- send_index: int32 [32, 8, 32, 512], P('region'), may hold values from 0 to 4095
- block_index: int32 [32, 8, 16, 2048], P('region', 'member'), may hold values from 0 to 16383
- block_count: int32 [32, 8, 16], P('region', 'member'), may hold values from 1 to 2048, as said below
- taper_index: int32 [32, 8, 16, 2048], P('region', 'member'), may hold values from 0 to 63
Outputs:
- analysis: bfloat16 [128, 4096, 512], P('member', 'region')
The draws below stay inside these ranges and needn't reach their ends.
Inputs may be any that keep to these rules, and one draw needn't show every extreme that they name: `send_index`: local observation numbers of the sending region. `block_index`: positions in the pool of 16384 observations that the column's device receives, region of anchor major. `block_count`: some column has exactly 2048 live observations in every draw; regions differ in their density of observations.
All inputs are finite; a program needn't handle non-finite values.
Results may differ from the reference program's by a relative error of at most 0.0065.
Values may be sent and summed in bfloat16 or wider, within the bound.
A program may use at most 128 MiB of HBM per device.

```python
import math
import jax
import jax.numpy as jnp
from jax import lax

K = 128
CV = 512
COL_DEV = 128
OBS_DEV = 4096
SLOT = 512
NLOC = 2048
NTAPER = 64
NS_ITERS = 6
CP = 16
NCOL = 4096
NOBS = 131072
N_MEMBER = 8
N_REGION = 32


def draw_block_count(key, part):
    key_base = jax.random.fold_in(key, 11)
    key_heavy = jax.random.fold_in(key, 12)
    key_spot = jax.random.fold_in(key, 13)
    base_counts = jax.random.randint(key_base, (N_REGION, N_MEMBER, CP), NLOC // 4, NLOC + 1)
    density = jax.random.randint(key_heavy, (N_REGION, 1, 1), 1, 5)
    counts = jnp.maximum(base_counts * density // 4, 1)
    chosen = jax.random.randint(key_spot, (), 0, N_REGION * N_MEMBER * CP)
    flat_counts = counts.reshape(-1)
    flat_counts = jnp.where(jnp.arange(flat_counts.shape[0]) == chosen, NLOC, flat_counts)
    return flat_counts.reshape(counts.shape).astype(jnp.int32)


def plant(values, rng, smallest, high):
    longest = values.shape.index(max(values.shape))
    spots = []
    for shift in (0, 1):
        where = [jax.random.randint(jax.random.fold_in(rng, axis), (), 0, length) for axis, length in enumerate(values.shape)]
        where[longest] = (where[longest] + shift) % values.shape[longest]
        spots.append(tuple(where))
    return values.at[spots[0]].set(smallest).at[spots[1]].set(high)


def block_scale(key, dims, pieces, smallest, high):
    def one(position, blocks):
        heights = jax.random.uniform(jax.random.fold_in(jax.random.fold_in(key, 6), position), (blocks,), jnp.float32, smallest / len(pieces), high / len(pieces))
        return jnp.repeat(jnp.exp(heights), dims[position] // blocks).reshape((-1,) + (1,) * (len(dims) - position - 1))

    gain = one(*pieces[0])
    for cut in pieces[1:]:
        gain = gain * one(*cut)
    return gain


def scatter_about(key, extent, deviation, bound, split=(), kind=jnp.bfloat16):
    level = block_scale(key, extent, split, -0.22, 0.18) if split else 1.0
    values = jax.random.normal(key, extent, jnp.float32) * deviation * level
    return jnp.minimum(jnp.maximum(values, -bound), bound).astype(kind)


def setup_inputs(seed: int = 0) -> dict:
    key_list = jax.random.split(jax.random.key(seed), 9)
    return {
        "background": scatter_about(key_list[0], (K, NCOL, CV), 1.0, 6.0, ((0, 8), (1, 32))),
        "obs_anom": scatter_about(key_list[1], (K, NOBS), 1.0, 6.0, ((0, 8), (1, 32))),
        "innovation": scatter_about(key_list[2], (NOBS,), 1.0, 6.0, ((0, 32),), jnp.float32),
        "obs_error": jnp.clip(jnp.exp(math.log(2.0) - 1.3862944 * jax.random.uniform(key_list[3], (NOBS,), jnp.float32) ** block_scale(key_list[3], (NOBS,), ((0, 32),), -0.2, 0.2)), 0.5, 2.0),
        "send_index": plant(jax.random.randint(key_list[4], (N_REGION, N_MEMBER, N_REGION, SLOT), 0, OBS_DEV), jax.random.fold_in(key_list[4], 1), 0, OBS_DEV - 1).astype(jnp.int32),
        "block_index": plant(jax.random.randint(key_list[5], (N_REGION, N_MEMBER, CP, NLOC), 0, N_REGION * SLOT), jax.random.fold_in(key_list[5], 1), 0, (N_REGION * SLOT) - 1).astype(jnp.int32),
        "block_count": draw_block_count(jax.random.fold_in(key_list[8], 71), 0),
        "taper_index": plant(jax.random.randint(key_list[7], (N_REGION, N_MEMBER, CP, NLOC), 0, NTAPER), jax.random.fold_in(key_list[7], 1), 0, NTAPER - 1).astype(jnp.int32),
    }


HIGHEST_PREC = lax.Precision.HIGHEST

def taper_weights(taper_index, block_count):
    radius = 2.0 * (taper_index.astype(jnp.float32) + 0.5) / NTAPER
    inside_part = 1.0 - 5.0 / 3.0 * radius ** 2 + 0.625 * radius ** 3 + 0.5 * radius ** 4 - 0.25 * radius ** 5
    outside_part = 4.0 - 5.0 * radius + 5.0 / 3.0 * radius ** 2 + 0.625 * radius ** 3 - 0.5 * radius ** 4 + radius ** 5 / 12.0 - 2.0 / (3.0 * radius)
    weight = jnp.maximum(jnp.where(radius < 1.0, inside_part, outside_part), 0.0)
    places = lax.broadcasted_iota(jnp.int32, taper_index.shape, taper_index.ndim - 1)
    return jnp.where(places < block_count[..., None], weight, 0.0)

def column_transforms(obs_rows, obs_dev, weights):
    members = obs_rows.shape[0]
    root_weight = jnp.sqrt(weights)
    local_rows = (root_weight[None] * obs_rows.astype(jnp.float32)).astype(jnp.bfloat16)
    local_rows = lax.optimization_barrier(local_rows).astype(jnp.float32)
    scaled_dev = root_weight * obs_dev
    identity = jnp.eye(members, dtype=jnp.float32)
    gram_mat = jnp.einsum('abl,cbl->bac', local_rows, local_rows, precision=HIGHEST_PREC) + (members - 1.0) * identity
    projected = jnp.einsum('abl,bl->ba', local_rows, scaled_dev, precision=HIGHEST_PREC)
    frob_norm = jnp.sqrt(lax.optimization_barrier(jnp.sum(gram_mat * gram_mat, axis=(1, 2))))
    iterate = gram_mat / frob_norm[:, None, None]
    inverse_root = jnp.broadcast_to(identity, gram_mat.shape)
    for sweep_num in range(NS_ITERS):
        factor = 1.5 * identity - 0.5 * jnp.einsum('bij,bjk->bik', inverse_root, iterate, precision=HIGHEST_PREC)
        iterate = jnp.einsum('bij,bjk->bik', iterate, factor, precision=HIGHEST_PREC)
        inverse_root = jnp.einsum('bij,bjk->bik', factor, inverse_root, precision=HIGHEST_PREC)
    weights_mat = jnp.sqrt(members - 1.0) * inverse_root / jnp.sqrt(frob_norm)[:, None, None]
    half_step = jnp.einsum('bij,bj->bi', inverse_root, projected, precision=HIGHEST_PREC)
    mean_shift = jnp.einsum('bij,bj->bi', inverse_root, half_step, precision=HIGHEST_PREC) / frob_norm[:, None]
    return (weights_mat + mean_shift[:, :, None]).astype(jnp.bfloat16)

def analysis_block(ensemble, transform):
    mean_state = lax.optimization_barrier(jnp.mean(ensemble.astype(jnp.float32), axis=0))
    anomalies = (ensemble.astype(jnp.float32) - mean_state).astype(jnp.bfloat16)
    anomalies = lax.optimization_barrier(anomalies).astype(jnp.float32)
    combined = jnp.einsum('jcv,cjk->kcv', anomalies, transform.astype(jnp.float32), precision=HIGHEST_PREC)
    return (mean_state + combined).astype(jnp.bfloat16)

def reference(background, obs_anom, innovation, obs_error, send_index, block_index, block_count, taper_index):
    scaled = (obs_anom.astype(jnp.float32) / obs_error[None, :]).astype(jnp.bfloat16)
    dscaled = (innovation / obs_error).astype(jnp.bfloat16)
    source = (block_index // SLOT).astype(jnp.int32)
    within = (block_index % SLOT).astype(jnp.int32)
    region_ids = jnp.arange(N_REGION, dtype=jnp.int32)[:, None, None, None]
    member_ids = jnp.arange(N_MEMBER, dtype=jnp.int32)[None, :, None, None]
    local_ids = send_index[source, member_ids, region_ids, within]
    obs_ids = (source * OBS_DEV + local_ids).astype(jnp.int32).reshape(N_REGION, COL_DEV, NLOC)
    weights = taper_weights(taper_index, block_count).reshape(N_REGION, COL_DEV, NLOC)
    state_blocks = background.reshape(K, N_REGION, COL_DEV, CV).transpose(1, 0, 2, 3)

    def one_region(packed):
        region_obs, region_weights, region_state = packed
        obs_rows = jnp.take(scaled, region_obs, axis=1)
        obs_dev = dscaled[region_obs].astype(jnp.float32)
        transform = column_transforms(obs_rows, obs_dev, region_weights)
        return analysis_block(region_state, transform)
    result = lax.map(one_region, (obs_ids, weights, state_blocks))
    return result.transpose(1, 0, 2, 3).reshape(K, NCOL, CV)
```

```python
import functools

import jax
import jax.numpy as jnp
from jax import lax
from jax.experimental import pallas as pl
from jax.experimental.pallas import tpu as pltpu
from jax.sharding import PartitionSpec as P

K = 128
SLOT = 512
NTAPER = 64
NS_ITERS = 6
LANES = 128
CGROUP = 4

NT = (((1,), (1,)), ((), ()))
VMEM_SPEC = pl.BlockSpec(memory_space=pltpu.VMEM)
SMEM_SPEC = pl.BlockSpec(memory_space=pltpu.SMEM)
PARAMS = pltpu.CompilerParams(vmem_limit_bytes=56 * 2**20)


def taper_weights(taper_index, block_count):
    radius = 2.0 * (taper_index.astype(jnp.float32) + 0.5) / NTAPER
    r2 = radius * radius
    r3 = r2 * radius
    r4 = r2 * r2
    r5 = r4 * radius
    inside_part = 1.0 - 5.0 / 3.0 * r2 + 0.625 * r3 + 0.5 * r4 - 0.25 * r5
    outside_part = (
        4.0 - 5.0 * radius + 5.0 / 3.0 * r2 + 0.625 * r3 - 0.5 * r4 + r5 / 12.0
        - 2.0 / (3.0 * radius)
    )
    weight = jnp.maximum(jnp.where(radius < 1.0, inside_part, outside_part), 0.0)
    places = lax.broadcasted_iota(jnp.int32, taper_index.shape, 1)
    return jnp.where(places < block_count, weight, 0.0)


def gather_kernel(idx_smem, idx_ref, obs_ref, err_ref, innov2_ref, err2_ref, out_ref, dev_ref,
                  table, rows):
    regions = idx_ref.shape[0]
    obs_count = obs_ref.shape[1]
    for q in range(obs_count // SLOT):
        cols = pl.ds(q * SLOT, SLOT)
        scaled = (obs_ref[:, cols].astype(jnp.float32) / err_ref[:, cols]).astype(jnp.bfloat16)
        table[cols, :] = scaled.astype(jnp.float32).T
    dscaled = (innov2_ref[...] / err2_ref[...]).astype(jnp.bfloat16)

    def block(r, _):
        base = r * SLOT

        def body(g, _):
            first = pl.multiple_of(g * 32, 32)
            for j in range(32):
                rows[pl.ds(first + j, 1), :] = table[pl.ds(idx_smem[base + first + j], 1), :]
            return 0

        lax.fori_loop(0, SLOT // 32, body, 0)
        out_ref[r] = rows[...].T.astype(jnp.bfloat16)
        dev_ref[r] = dev_pick(idx_ref[r], dscaled)
        return 0

    lax.fori_loop(0, regions, block, 0)


def dev_pick(idx, dscaled):
    low = lax.broadcasted_iota(jnp.int32, (LANES, SLOT), 0) == (idx & (LANES - 1))
    picked = jnp.dot(
        dscaled, low.astype(jnp.float32).astype(jnp.bfloat16), preferred_element_type=jnp.float32
    )
    high = lax.broadcasted_iota(jnp.int32, picked.shape, 0) == (idx >> 7)
    return jnp.sum(jnp.where(high, picked, 0.0), axis=0, keepdims=True)


def gather_blocks(wanted, obs_full, innovation, obs_error):
    regions = wanted.shape[0]
    obs_count = obs_full.shape[1]
    return pl.pallas_call(
        gather_kernel,
        out_shape=(
            jax.ShapeDtypeStruct((regions, K, SLOT), jnp.bfloat16),
            jax.ShapeDtypeStruct((regions, 1, SLOT), jnp.float32),
        ),
        in_specs=[SMEM_SPEC] + [VMEM_SPEC] * 5,
        out_specs=(VMEM_SPEC, VMEM_SPEC),
        scratch_shapes=[
            pltpu.VMEM((obs_count, K), jnp.float32),
            pltpu.VMEM((SLOT, K), jnp.float32),
        ],
        compiler_params=PARAMS,
        cost_estimate=pl.CostEstimate(flops=10**9, bytes_accessed=6 * 2**20, transcendentals=0),
    )(
        wanted.reshape(-1),
        wanted.reshape(regions, 1, SLOT),
        obs_full,
        obs_error.reshape(1, obs_count),
        innovation.reshape(-1, LANES),
        obs_error.reshape(-1, LANES),
    )


def split(x):
    high = x.astype(jnp.bfloat16)
    low = (x - high.astype(jnp.float32)).astype(jnp.bfloat16)
    return high, low


def dot3(a, b):
    ah, al = a
    bh, bl = b
    return jnp.dot(
        jnp.concatenate([ah, al, ah], axis=1),
        jnp.concatenate([bh, bh, bl], axis=0),
        preferred_element_type=jnp.float32,
    )


def scatter_weights(c, bidx_ref, rho, wmat):
    p = bidx_ref[c]
    weight = rho[c]
    count = p.shape[1]
    rows = lax.broadcasted_iota(jnp.int32, (LANES, count), 0)
    first = (rows == (p >> 7)).astype(jnp.float32).astype(jnp.bfloat16)
    high = weight.astype(jnp.bfloat16).astype(jnp.float32)
    hit = rows == (p & (LANES - 1))
    second = jnp.concatenate(
        [
            jnp.where(hit, high, 0.0).astype(jnp.bfloat16),
            jnp.where(hit, weight - high, 0.0).astype(jnp.bfloat16),
        ],
        axis=0,
    )
    both = lax.dot_general(first, second, NT, preferred_element_type=jnp.float32)
    wmat[c] = both[:, :LANES] + both[:, LANES:]


def gram_block(r, block, dev, wmat, weighted, right, acc):
    columns = wmat.shape[0]
    lead = SLOT // LANES
    values = block.astype(jnp.float32)
    right[0:K, :] = block
    first = lax.broadcasted_iota(jnp.int32, (16, SLOT), 0) == 0
    right[K : K + 16, :] = jnp.where(first, dev, 0.0).astype(jnp.bfloat16)
    for c in range(columns):
        for q in range(lead):
            lanes = slice(q * LANES, (q + 1) * LANES)
            w = wmat[c, pl.ds(r * lead + q, 1), :]
            weighted[c * K : (c + 1) * K, lanes] = (values[:, lanes] * w).astype(jnp.bfloat16)
    acc[...] += lax.dot_general(
        weighted[...], right[...], NT, preferred_element_type=jnp.float32
    )


def eye():
    shape = (K, K)
    same = lax.broadcasted_iota(jnp.int32, shape, 0) == lax.broadcasted_iota(jnp.int32, shape, 1)
    return same.astype(jnp.float32)


def transforms(grams):
    identity = eye()
    members = float(K)
    mats = [g[:, :K] + (members - 1.0) * identity for g in grams]
    norms = [jnp.sqrt(jnp.sum(m * m, axis=(0, 1), keepdims=True)) for m in mats]
    ys = [m / n for m, n in zip(mats, norms)]
    zs = [1.5 * identity - 0.5 * y for y in ys]
    ys = [dot3(split(z), split(y)) for z, y in zip(zs, ys)]
    for sweep in range(1, NS_ITERS):
        sy = [split(y) for y in ys]
        sz = [split(z) for z in zs]
        sf = [split(1.5 * identity - 0.5 * dot3(z, y)) for z, y in zip(sz, sy)]
        if sweep == NS_ITERS - 1:
            zs = [dot3(f, z) for f, z in zip(sf, sz)]
        else:
            both = [
                dot3(f, tuple(jnp.concatenate([a, b], axis=1) for a, b in zip(y, z)))
                for f, y, z in zip(sf, sy, sz)
            ]
            ys = [b[:, :K] for b in both]
            zs = [b[:, K:] for b in both]
    sz = [split(z) for z in zs]
    half = [dot3(z, split(g[:, K:])) for z, g in zip(sz, grams)]
    full = [dot3(z, split(h)) for z, h in zip(sz, half)]
    out = []
    for z, f, n in zip(zs, full, norms):
        out.append(jnp.sqrt(members - 1.0) * z / jnp.sqrt(n) + f[:, 0:1] / n)
    return out


def analyse(c, transform, bg_ref, out_ref):
    state = bg_ref[:, c].reshape(K, bg_ref.shape[3]).astype(jnp.float32)
    mean_state = jnp.sum(state, axis=0, keepdims=True) * (1.0 / K)
    anomalies = (state - mean_state).astype(jnp.bfloat16)
    combined = jnp.dot(
        transform.T.astype(jnp.bfloat16), anomalies, preferred_element_type=jnp.float32
    )
    result = (mean_state + combined).astype(jnp.bfloat16)
    out_ref[:, c] = result.reshape(out_ref.shape[0], out_ref.shape[2], out_ref.shape[3])


def column_kernel(pool_ref, dev_ref, bidx_ref, taper_ref, count_ref, bg_ref, out_ref,
                  wmat, rho, weighted, right, acc):
    columns = bidx_ref.shape[0]
    regions = pool_ref.shape[0]
    for c in range(columns):
        rho[c] = taper_weights(taper_ref[c], count_ref[c])
    lax.fori_loop(0, columns, lambda c, _: (scatter_weights(c, bidx_ref, rho, wmat), 0)[1], 0)
    acc[...] = jnp.zeros_like(acc)
    right[...] = jnp.zeros_like(right)

    def one_block(r, _):
        gram_block(r, pool_ref[r], dev_ref[r], wmat, weighted, right, acc)
        return 0

    lax.fori_loop(0, regions, one_block, 0)

    def group(g, _):
        first = g * CGROUP
        grams = [acc[pl.ds((first + i) * K, K), :] for i in range(CGROUP)]
        for i, t in enumerate(transforms(grams)):
            analyse(first + i, t, bg_ref, out_ref)
        return 0

    lax.fori_loop(0, columns // CGROUP, group, 0)


def analyse_columns(pool, dev, block_rows, taper_index, block_count, state):
    columns, places = block_rows.shape
    return pl.pallas_call(
        column_kernel,
        out_shape=jax.ShapeDtypeStruct(state.shape, jnp.bfloat16),
        in_specs=[VMEM_SPEC] * 4 + [SMEM_SPEC, VMEM_SPEC],
        out_specs=VMEM_SPEC,
        scratch_shapes=[
            pltpu.VMEM((columns, LANES, LANES), jnp.float32),
            pltpu.VMEM((columns, 1, places), jnp.float32),
            pltpu.VMEM((columns * K, SLOT), jnp.bfloat16),
            pltpu.VMEM((2 * K, SLOT), jnp.bfloat16),
            pltpu.VMEM((columns * K, 2 * K), jnp.float32),
        ],
        compiler_params=PARAMS,
        cost_estimate=pl.CostEstimate(
            flops=2 * 10**10, bytes_accessed=12 * 2**20, transcendentals=0
        ),
    )(
        pool,
        dev,
        block_rows.reshape(columns, 1, places),
        taper_index.reshape(columns, 1, places),
        block_count,
        state,
    )


def shards(
    background, obs_anom, innovation, obs_error, send_index, block_index, block_count, taper_index
):
    member_pos = lax.axis_index("member")
    member_count = lax.axis_size("member")
    own, columns_all, values = background.shape
    columns = columns_all // member_count
    wanted = lax.dynamic_index_in_dim(send_index[0], member_pos, 0, keepdims=False)
    obs_full = lax.all_gather(obs_anom, "member", axis=0, tiled=True)
    send, send_dev = gather_blocks(wanted, obs_full, innovation, obs_error)
    exchange = functools.partial(
        lax.all_to_all, axis_name="region", split_axis=0, concat_axis=0, tiled=True
    )
    pool = exchange(send)
    dev = exchange(send_dev)
    state = background.transpose(1, 0, 2).reshape(member_count, columns, own, values)
    trade = functools.partial(
        lax.all_to_all, axis_name="member", split_axis=0, concat_axis=0, tiled=True
    )
    state = trade(state)
    updated = analyse_columns(
        pool, dev, block_index[0, 0], taper_index[0, 0], block_count[0, 0], state
    )
    result = trade(updated)
    return result.reshape(columns_all, own, values).transpose(1, 0, 2)


def solution(mesh):
    in_specs = (
        P("member", "region", None),
        P("member", "region"),
        P("region"),
        P("region"),
        P("region", None, None, None),
        P("region", "member", None, None),
        P("region", "member", None),
        P("region", "member", None, None),
    )
    out_specs = P("member", "region", None)
    return jax.shard_map(shards, mesh=mesh, in_specs=in_specs, out_specs=out_specs, check_vma=False)
```

```python
import jax
import jax.numpy as jnp
from jax import lax
from jax.experimental import pallas as pl
from jax.experimental.pallas import tpu as pltpu
from jax.sharding import PartitionSpec as P

K = 128
SLOT = 512
NTAPER = 64
NS_ITERS = 6
LANES = 128
CGROUP = 4
MEMBERS = 8
REGIONS = 32
NZ = 8
NY = 4
BLOCKS = 30
MESH = pl.DeviceIdType.MESH

NT = (((1,), (1,)), ((), ()))
VMEM_SPEC = pl.BlockSpec(memory_space=pltpu.VMEM)
SMEM_SPEC = pl.BlockSpec(memory_space=pltpu.SMEM)


def taper_weights(taper_index, block_count):
    radius = 2.0 * (taper_index.astype(jnp.float32) + 0.5) / NTAPER
    r2 = radius * radius
    r3 = r2 * radius
    r4 = r2 * r2
    r5 = r4 * radius
    inside_part = 1.0 - 5.0 / 3.0 * r2 + 0.625 * r3 + 0.5 * r4 - 0.25 * r5
    outside_part = (
        4.0 - 5.0 * radius + 5.0 / 3.0 * r2 + 0.625 * r3 - 0.5 * r4 + r5 / 12.0
        - 2.0 / (3.0 * radius)
    )
    weight = jnp.maximum(jnp.where(radius < 1.0, inside_part, outside_part), 0.0)
    places = lax.broadcasted_iota(jnp.int32, taper_index.shape, 1)
    return jnp.where(places < block_count, weight, 0.0)


def dev_pick(idx, dscaled):
    low = lax.broadcasted_iota(jnp.int32, (LANES, SLOT), 0) == (idx & (LANES - 1))
    picked = jnp.dot(
        dscaled, low.astype(jnp.float32).astype(jnp.bfloat16), preferred_element_type=jnp.float32
    )
    high = lax.broadcasted_iota(jnp.int32, picked.shape, 0) == (idx >> 7)
    return jnp.sum(jnp.where(high, picked, 0.0), axis=0, keepdims=True)


def split(x):
    high = x.astype(jnp.bfloat16)
    low = (x - high.astype(jnp.float32)).astype(jnp.bfloat16)
    return high, low


def dot3(a, b):
    ah, al = a
    bh, bl = b
    return jnp.dot(
        jnp.concatenate([ah, al, ah], axis=1),
        jnp.concatenate([bh, bh, bl], axis=0),
        preferred_element_type=jnp.float32,
    )


def scatter_weights(c, bidx_ref, rho, wmat):
    p = bidx_ref[pl.ds(c, 1), :]
    weight = rho[pl.ds(c, 1), :]
    count = p.shape[1]
    rows = lax.broadcasted_iota(jnp.int32, (LANES, count), 0)
    first = (rows == (p >> 7)).astype(jnp.float32).astype(jnp.bfloat16)
    high = weight.astype(jnp.bfloat16).astype(jnp.float32)
    hit = rows == (p & (LANES - 1))
    second = jnp.concatenate(
        [
            jnp.where(hit, high, 0.0).astype(jnp.bfloat16),
            jnp.where(hit, weight - high, 0.0).astype(jnp.bfloat16),
        ],
        axis=0,
    )
    both = lax.dot_general(first, second, NT, preferred_element_type=jnp.float32)
    wmat[c] = both[:, :LANES] + both[:, LANES:]


def gram_block(r, block, dev, wmat, weighted, right, acc):
    columns = wmat.shape[0]
    lead = SLOT // LANES
    values = block.astype(jnp.float32)
    right[0:K, :] = block
    first = lax.broadcasted_iota(jnp.int32, (16, SLOT), 0) == 0
    right[K : K + 16, :] = jnp.where(first, dev, 0.0).astype(jnp.bfloat16)
    for c in range(columns):
        for q in range(lead):
            lanes = slice(q * LANES, (q + 1) * LANES)
            w = wmat[c, pl.ds(r * lead + q, 1), :]
            weighted[c * K : (c + 1) * K, lanes] = (values[:, lanes] * w).astype(jnp.bfloat16)
    acc[...] += lax.dot_general(
        weighted[...], right[...], NT, preferred_element_type=jnp.float32
    )


def eye():
    shape = (K, K)
    same = lax.broadcasted_iota(jnp.int32, shape, 0) == lax.broadcasted_iota(jnp.int32, shape, 1)
    return same.astype(jnp.float32)


def transforms(grams):
    identity = eye()
    members = float(K)
    mats = [g[:, :K] + (members - 1.0) * identity for g in grams]
    norms = [jnp.sqrt(jnp.sum(m * m, axis=(0, 1), keepdims=True)) for m in mats]
    ys = [m / n for m, n in zip(mats, norms)]
    zs = [1.5 * identity - 0.5 * y for y in ys]
    ys = [dot3(split(z), split(y)) for z, y in zip(zs, ys)]
    for sweep in range(1, NS_ITERS):
        sy = [split(y) for y in ys]
        sz = [split(z) for z in zs]
        sf = [split(1.5 * identity - 0.5 * dot3(z, y)) for z, y in zip(sz, sy)]
        if sweep == NS_ITERS - 1:
            zs = [dot3(f, z) for f, z in zip(sf, sz)]
        else:
            both = [
                dot3(f, tuple(jnp.concatenate([a, b], axis=1) for a, b in zip(y, z)))
                for f, y, z in zip(sf, sy, sz)
            ]
            ys = [b[:, :K] for b in both]
            zs = [b[:, K:] for b in both]
    sz = [split(z) for z in zs]
    half = [dot3(z, split(g[:, K:])) for z, g in zip(sz, grams)]
    full = [dot3(z, split(h)) for z, h in zip(sz, half)]
    out = []
    for z, f, n in zip(zs, full, norms):
        out.append(jnp.sqrt(members - 1.0) * z / jnp.sqrt(n) + f[:, 0:1] / n)
    return out


def analyse(c, transform, bg_ref, out_ref):
    state = bg_ref[:, c].reshape(K, bg_ref.shape[3]).astype(jnp.float32)
    mean_state = jnp.sum(state, axis=0, keepdims=True) * (1.0 / K)
    anomalies = (state - mean_state).astype(jnp.bfloat16)
    combined = jnp.dot(
        transform.T.astype(jnp.bfloat16), anomalies, preferred_element_type=jnp.float32
    )
    result = (mean_state + combined).astype(jnp.bfloat16)
    out_ref[:, c] = result.reshape(out_ref.shape[0], out_ref.shape[2], out_ref.shape[3])


def place(j):
    block = j + j // 24 + j // 27
    combo, dy = block // 4, block % 4
    distance = 2 - (combo + 2) // 4
    dz = distance * (1 - 2 * (combo % 2))
    slot = combo // 4 - combo // 7
    return slot, dz, dy


def region_at(z, y):
    return ((z + 16) % NZ) * NY + (y + 8) % NY


def kernel(idx_smem, idx_ref, obs_ref, err_ref, innov2_ref, err2_ref, bidx_ref, taper_ref,
           count_ref, bg_ref, out_ref,
           own, full, pair, dev2, table, rows, sent, sent_dev, pool, pool_dev, state, result,
           wmat, rho, weighted, right, acc,
           obs_send, obs_recv, pair_send, pair_recv, bg_send, bg_recv,
           pool_send, pool_recv, dev_send, dev_recv, out_send, out_recv):
    me = lax.axis_index("member")
    region = lax.axis_index("region")
    z, y = region // NY, region % NY
    partner = region_at(z + 4, y)
    columns = bidx_ref.shape[0]
    obs_count = obs_ref.shape[1]
    others = [lax.rem(me + k, MEMBERS) for k in range(1, MEMBERS)]

    barrier = pltpu.get_barrier_semaphore()
    for other in others:
        pl.semaphore_signal(barrier, inc=1, device_id={"member": other}, device_id_type=MESH)
    pl.semaphore_signal(barrier, inc=1, device_id={"region": partner}, device_id_type=MESH)
    near = [(dz, dy) for dz in (-2, -1, 0, 1, 2) for dy in range(NY) if (dz, dy) != (0, 0)]
    for dz, dy in near:
        pl.semaphore_signal(
            barrier, inc=1, device_id={"region": region_at(z + dz, y + dy)}, device_id_type=MESH
        )
    own[...] = (obs_ref[...].astype(jnp.float32) / err_ref[...]).astype(jnp.bfloat16)
    dev2[0] = (innov2_ref[...] / err2_ref[...]).astype(jnp.bfloat16)
    pl.semaphore_wait(barrier, len(others) + 1 + len(near))

    def remote(src, dst, send, recv, where):
        return pltpu.make_async_remote_copy(
            src_ref=src, dst_ref=dst, send_sem=send, recv_sem=recv,
            device_id=where, device_id_type=MESH,
        )

    def pair_copy():
        return remote(own, pair, pair_send.at[0], pair_recv.at[0], {"region": partner})

    def pair_dev_copy():
        return remote(dev2.at[0], dev2.at[1], pair_send.at[1], pair_recv.at[1],
                      {"region": partner})

    def obs_copy(src, slot, owner, to):
        return remote(src, full.at[slot, owner], obs_send.at[slot, to], obs_recv.at[slot, owner],
                      {"member": to})

    def bg_copy(owner, to):
        return remote(bg_ref.at[to], state.at[owner], bg_send.at[to], bg_recv.at[owner],
                      {"member": to})

    def block_copy(j, source, to):
        return remote(sent.at[j], pool.at[source], pool_send.at[j], pool_recv.at[source],
                      {"region": to})

    def block_dev_copy(j, source, to):
        return remote(sent_dev.at[j], pool_dev.at[source], dev_send.at[j], dev_recv.at[source],
                      {"region": to})

    def out_copy(g, owner, to):
        cols = pl.ds(g * CGROUP, CGROUP)
        return remote(result.at[to, cols], out_ref.at[owner, cols], out_send.at[g, to],
                      out_recv.at[g, owner], {"member": to})

    pair_copy().start()
    pair_dev_copy().start()
    for other in others:
        obs_copy(own, 0, me, other).start()
    full[0, me] = own[...]

    for c in range(columns):
        rho[pl.ds(c, 1), :] = taper_weights(taper_ref[pl.ds(c, 1), :], count_ref[c])
    half = columns // 2
    scatter = lambda c, _: (scatter_weights(c, bidx_ref, rho, wmat), 0)[1]
    lax.fori_loop(0, half, scatter, 0)
    acc[...] = jnp.zeros_like(acc)
    right[...] = jnp.zeros_like(right)

    pair_copy().wait_recv()
    for other in others:
        obs_copy(pair, 1, me, other).start()
    full[1, me] = pair[...]
    for other in others:
        bg_copy(me, other).start()
    keep_bg = pltpu.make_async_copy(bg_ref.at[me], state.at[me], bg_send.at[me])
    keep_bg.start()
    lax.fori_loop(half, columns, scatter, 0)
    pair_dev_copy().wait_recv()

    def build(slot):
        for other in others:
            obs_copy(own, slot, other, other).wait_recv()
        for q in range(obs_count // SLOT):
            part = full[slot, :, :, q * SLOT : (q + 1) * SLOT]
            part = part.reshape(K, SLOT).astype(jnp.float32)
            table[pl.ds(slot * obs_count + q * SLOT, SLOT), :] = part.T

    def gather(slot, to):
        base = (slot * REGIONS + to) * SLOT
        start = slot * obs_count

        def body(g, _):
            first = pl.multiple_of(g * 32, 32)
            for j in range(32):
                at = idx_smem[base + first + j] + start
                rows[pl.ds(first + j, 1), :] = table[pl.ds(at, 1), :]
            return 0

        lax.fori_loop(0, SLOT // 32, body, 0)
        picked = dev_pick(idx_ref[slot, pl.ds(to, 1), :], dev2[slot])
        return rows[...].T.astype(jnp.bfloat16), picked

    def send(j, _):
        slot, dz, dy = place(j)
        to = region_at(z + dz, y + dy)
        source = region_at(z + 4 * slot, y)
        block, dev = gather(slot, to)
        sent[j] = block
        sent_dev[j] = dev
        block_copy(j, source, to).start()
        block_dev_copy(j, source, to).start()
        return 0

    build(0)
    lax.fori_loop(0, 16, send, 0)
    build(1)
    lax.fori_loop(16, BLOCKS, send, 0)
    for slot in range(2):
        source = region_at(z + 4 * slot, y)
        block, dev = gather(slot, region)
        gram_block(source, block, dev, wmat, weighted, right, acc)

    def receive(j, _):
        slot, dz, dy = place(j)
        source = region_at(z - dz + 4 * slot, y - dy)
        block_copy(j, source, region).wait_recv()
        block_dev_copy(j, source, region).wait_recv()
        gram_block(source, pool[source], pool_dev[source], wmat, weighted, right, acc)
        return 0

    lax.fori_loop(0, BLOCKS, receive, 0)
    keep_bg.wait()
    for other in others:
        bg_copy(other, other).wait_recv()

    def group(g, _):
        first = g * CGROUP
        grams = [acc[pl.ds((first + i) * K, K), :] for i in range(CGROUP)]
        for i, t in enumerate(transforms(grams)):
            analyse(first + i, t, state, result)
        for other in others:
            out_copy(g, me, other).start()
        cols = pl.ds(first, CGROUP)
        pltpu.make_async_copy(result.at[me, cols], out_ref.at[me, cols], out_send.at[g, me]).start()
        return 0

    groups = columns // CGROUP
    lax.fori_loop(0, groups, group, 0)

    pair_copy().wait_send()
    pair_dev_copy().wait_send()
    for other in others:
        obs_copy(own, 0, me, other).wait_send()
        obs_copy(pair, 1, me, other).wait_send()
        bg_copy(me, other).wait_send()

    def drain(j, _):
        block_copy(j, region, region).wait_send()
        block_dev_copy(j, region, region).wait_send()
        return 0

    lax.fori_loop(0, BLOCKS, drain, 0)

    def finish(g, _):
        cols = pl.ds(g * CGROUP, CGROUP)
        for other in others:
            out_copy(g, me, other).wait_send()
            out_copy(g, other, other).wait_recv()
        pltpu.make_async_copy(result.at[me, cols], out_ref.at[me, cols], out_send.at[g, me]).wait()
        return 0

    lax.fori_loop(0, groups, finish, 0)


def assimilate(wanted, obs_anom, innovation, obs_error, block_rows, taper_index, block_count,
               state):
    columns, places = block_rows.shape
    own, obs_count = obs_anom.shape
    values = state.shape[3]
    groups = columns // CGROUP
    bf16, f32 = jnp.bfloat16, jnp.float32
    dma = pltpu.SemaphoreType.DMA
    return pl.pallas_call(
        kernel,
        out_shape=jax.ShapeDtypeStruct(state.shape, bf16),
        in_specs=[SMEM_SPEC] + [VMEM_SPEC] * 7 + [SMEM_SPEC, pl.BlockSpec(memory_space=pl.ANY)],
        out_specs=pl.BlockSpec(memory_space=pl.ANY),
        scratch_shapes=[
            pltpu.VMEM((own, obs_count), bf16),
            pltpu.VMEM((2, MEMBERS, own, obs_count), bf16),
            pltpu.VMEM((own, obs_count), bf16),
            pltpu.VMEM((2, obs_count // LANES, LANES), bf16),
            pltpu.VMEM((2 * obs_count, K), f32),
            pltpu.VMEM((SLOT, K), f32),
            pltpu.VMEM((BLOCKS, K, SLOT), bf16),
            pltpu.VMEM((BLOCKS, 1, SLOT), f32),
            pltpu.VMEM((REGIONS, K, SLOT), bf16),
            pltpu.VMEM((REGIONS, 1, SLOT), f32),
            pltpu.VMEM((MEMBERS, columns, own, values), bf16),
            pltpu.VMEM((MEMBERS, columns, own, values), bf16),
            pltpu.VMEM((columns, LANES, LANES), f32),
            pltpu.VMEM((columns, places), f32),
            pltpu.VMEM((columns * K, SLOT), bf16),
            pltpu.VMEM((2 * K, SLOT), bf16),
            pltpu.VMEM((columns * K, 2 * K), f32),
            dma((2, MEMBERS)),
            dma((2, MEMBERS)),
            dma((2,)),
            dma((2,)),
            dma((MEMBERS,)),
            dma((MEMBERS,)),
            dma((BLOCKS,)),
            dma((REGIONS,)),
            dma((BLOCKS,)),
            dma((REGIONS,)),
            dma((groups, MEMBERS)),
            dma((groups, MEMBERS)),
        ],
        compiler_params=pltpu.CompilerParams(
            vmem_limit_bytes=56 * 2**20, collective_id=0, has_side_effects=True
        ),
        cost_estimate=pl.CostEstimate(
            flops=2 * 10**10, bytes_accessed=12 * 2**20, transcendentals=0
        ),
    )(
        wanted.reshape(-1),
        wanted,
        obs_anom,
        obs_error.reshape(1, obs_count),
        innovation.reshape(-1, LANES),
        obs_error.reshape(-1, LANES),
        block_rows,
        taper_index,
        block_count,
        state,
    )


def shards(
    background, obs_anom, innovation, obs_error, send_index, block_index, block_count, taper_index
):
    own, columns_all, values = background.shape
    columns = columns_all // MEMBERS
    wanted = lax.dynamic_index_in_dim(send_index[0], lax.axis_index("member"), 0, keepdims=False)
    across = [(r, (r + REGIONS // 2) % REGIONS) for r in range(REGIONS)]
    wanted = jnp.stack([wanted, lax.ppermute(wanted, "region", across)])
    state = background.transpose(1, 0, 2).reshape(MEMBERS, columns, own, values)
    result = assimilate(
        wanted, obs_anom, innovation, obs_error, block_index[0, 0], taper_index[0, 0],
        block_count[0, 0], state,
    )
    return result.reshape(columns_all, own, values).transpose(1, 0, 2)


def solution(mesh):
    in_specs = (
        P("member", "region", None),
        P("member", "region"),
        P("region"),
        P("region"),
        P("region", None, None, None),
        P("region", "member", None, None),
        P("region", "member", None),
        P("region", "member", None, None),
    )
    out_specs = P("member", "region", None)
    return jax.shard_map(shards, mesh=mesh, in_specs=in_specs, out_specs=out_specs, check_vma=False)
```

```python
import jax
import jax.numpy as jnp
from jax import lax
from jax.experimental import pallas as pl
from jax.experimental.pallas import tpu as pltpu
from jax.sharding import PartitionSpec as P

K = 128
SLOT = 512
NTAPER = 64
NS_ITERS = 6
LANES = 128
CGROUP = 8
OGROUP = 4
MEMBERS = 8
REGIONS = 32
NZ = 8
NY = 4
BLOCKS = 30
MESH = pl.DeviceIdType.MESH

NT = (((1,), (1,)), ((), ()))
VMEM_SPEC = pl.BlockSpec(memory_space=pltpu.VMEM)
SMEM_SPEC = pl.BlockSpec(memory_space=pltpu.SMEM)


def taper_weights(taper_index, block_count):
    radius = 2.0 * (taper_index.astype(jnp.float32) + 0.5) / NTAPER
    r2 = radius * radius
    r3 = r2 * radius
    r4 = r2 * r2
    r5 = r4 * radius
    inside_part = 1.0 - 5.0 / 3.0 * r2 + 0.625 * r3 + 0.5 * r4 - 0.25 * r5
    outside_part = (
        4.0 - 5.0 * radius + 5.0 / 3.0 * r2 + 0.625 * r3 - 0.5 * r4 + r5 / 12.0
        - 2.0 / (3.0 * radius)
    )
    weight = jnp.maximum(jnp.where(radius < 1.0, inside_part, outside_part), 0.0)
    places = lax.broadcasted_iota(jnp.int32, taper_index.shape, 1)
    return jnp.where(places < block_count, weight, 0.0)


def dev_pick(idx, dscaled):
    low = lax.broadcasted_iota(jnp.int32, (LANES, SLOT), 0) == (idx & (LANES - 1))
    picked = jnp.dot(
        dscaled, low.astype(jnp.float32).astype(jnp.bfloat16), preferred_element_type=jnp.float32
    )
    high = lax.broadcasted_iota(jnp.int32, picked.shape, 0) == (idx >> 7)
    return jnp.sum(jnp.where(high, picked, 0.0), axis=0, keepdims=True)


def split(x):
    high = x.astype(jnp.bfloat16)
    low = (x - high.astype(jnp.float32)).astype(jnp.bfloat16)
    return high, low


def dot3(a, b):
    ah, al = a
    bh, bl = b
    return jnp.dot(
        jnp.concatenate([ah, al, ah], axis=1),
        jnp.concatenate([bh, bh, bl], axis=0),
        preferred_element_type=jnp.float32,
    )


def scatter_weights(c, bidx_ref, rho, wmat):
    p = bidx_ref[pl.ds(c, 1), :]
    weight = rho[pl.ds(c, 1), :]
    count = p.shape[1]
    rows = lax.broadcasted_iota(jnp.int32, (LANES, count), 0)
    first = (rows == (p >> 7)).astype(jnp.float32).astype(jnp.bfloat16)
    high = weight.astype(jnp.bfloat16).astype(jnp.float32)
    hit = rows == (p & (LANES - 1))
    second = jnp.concatenate(
        [
            jnp.where(hit, high, 0.0).astype(jnp.bfloat16),
            jnp.where(hit, weight - high, 0.0).astype(jnp.bfloat16),
        ],
        axis=0,
    )
    both = lax.dot_general(first, second, NT, preferred_element_type=jnp.float32)
    wmat[c] = both[:, :LANES] + both[:, LANES:]


def gram_blocks(parts, wmat, right, acc):
    columns = wmat.shape[0]
    lead = SLOT // LANES
    first = lax.broadcasted_iota(jnp.int32, (16, SLOT), 0) == 0
    values = []
    for b, (r, block, dev) in enumerate(parts):
        lanes = slice(b * SLOT, (b + 1) * SLOT)
        right[0:K, lanes] = block
        right[K : K + 16, lanes] = jnp.where(first, dev, 0.0).astype(jnp.bfloat16)
        values.append(block.astype(jnp.float32))
    for c in range(0, columns, 2):
        weighted = []
        for column in (c, c + 1):
            pieces = []
            for v, (r, block, dev) in zip(values, parts):
                for q in range(lead):
                    w = wmat[column, pl.ds(r * lead + q, 1), :]
                    pieces.append((v[:, q * LANES : (q + 1) * LANES] * w).astype(jnp.bfloat16))
            weighted.append(jnp.concatenate(pieces, axis=1))
        acc[:, c * K : (c + 2) * K] += lax.dot_general(
            right[...], jnp.concatenate(weighted, axis=0), NT, preferred_element_type=jnp.float32
        )


def eye():
    shape = (K, K)
    same = lax.broadcasted_iota(jnp.int32, shape, 0) == lax.broadcasted_iota(jnp.int32, shape, 1)
    return same.astype(jnp.float32)


def transforms(grams, shifts):
    identity = eye()
    members = float(K)
    mats = [g + (members - 1.0) * identity for g in grams]
    norms = [jnp.sqrt(jnp.sum(m * m, axis=(0, 1), keepdims=True)) for m in mats]
    ys = [m / n for m, n in zip(mats, norms)]
    zs = [1.5 * identity - 0.5 * y for y in ys]
    ys = [dot3(split(z), split(y)) for z, y in zip(zs, ys)]
    for sweep in range(1, NS_ITERS):
        sy = [split(y) for y in ys]
        sz = [split(z) for z in zs]
        sf = [split(1.5 * identity - 0.5 * dot3(z, y)) for z, y in zip(sz, sy)]
        if sweep == NS_ITERS - 1:
            zs = [dot3(f, z) for f, z in zip(sf, sz)]
        else:
            both = [
                dot3(f, tuple(jnp.concatenate([a, b], axis=1) for a, b in zip(y, z)))
                for f, y, z in zip(sf, sy, sz)
            ]
            ys = [b[:, :K] for b in both]
            zs = [b[:, K:] for b in both]
    sz = [split(z) for z in zs]
    half = [dot3(split(p), z) for z, p in zip(sz, shifts)]
    full = [dot3(split(h), z) for z, h in zip(sz, half)]
    out = []
    for z, f, n in zip(zs, full, norms):
        out.append(jnp.sqrt(members - 1.0) * z / jnp.sqrt(n) + f[0:1, :] / n)
    return out


def analyse(c, transform, bg_ref, out_ref):
    state = bg_ref[:, c].reshape(K, bg_ref.shape[3]).astype(jnp.float32)
    mean_state = jnp.sum(state, axis=0, keepdims=True) * (1.0 / K)
    anomalies = (state - mean_state).astype(jnp.bfloat16)
    combined = jnp.dot(
        transform.astype(jnp.bfloat16), anomalies, preferred_element_type=jnp.float32
    )
    result = (mean_state + combined).astype(jnp.bfloat16)
    out_ref[:, c] = result.reshape(out_ref.shape[0], out_ref.shape[2], out_ref.shape[3])


def place(j):
    block = j + 2 * (j // 24)
    combo, dy = 2 * (block // 8) + block % 2, (block // 2) % 4
    distance = 2 - (combo + 2) // 4
    dz = distance * (1 - 2 * (combo % 2))
    slot = combo // 4 - combo // 7
    return slot, dz, dy


def region_at(z, y):
    return ((z + 16) % NZ) * NY + (y + 8) % NY


def permute_state(raw, state):
    count = raw.shape[1] * raw.shape[2]
    a = lax.broadcasted_iota(jnp.int32, (count, count), 0)
    b = lax.broadcasted_iota(jnp.int32, (count, count), 1)
    swap = (a // 16 == b % 16) & (a % 16 == b // 16)
    swap = swap.astype(jnp.float32).astype(jnp.bfloat16)
    for m in range(raw.shape[0]):
        rows = raw[m].reshape(count, raw.shape[3])
        moved = jnp.dot(swap, rows, preferred_element_type=jnp.float32).astype(jnp.bfloat16)
        state[m] = moved.reshape(state.shape[1:])


def kernel(send_ref, obs_ref, err_ref, innov2_ref, err2_ref, bidx_ref, taper_ref,
           count_ref, bg_ref, out_ref,
           idx_smem, idx_ref, own, full, pair, dev2, table, sent, sent_dev, pool, pool_dev,
           raw, state, result, wmat, rho, right, acc,
           idx_sem, obs_send, obs_recv, forward_send, pair_send, pair_recv, bg_send, bg_recv,
           pool_send, pool_recv, dev_send, dev_recv, out_send, out_recv):
    me = lax.axis_index("member")
    region = lax.axis_index("region")
    z, y = region // NY, region % NY
    partner = region_at(z + 4, y)
    columns = bidx_ref.shape[0]
    obs_count = obs_ref.shape[1]
    others = [lax.rem(me + k, MEMBERS) for k in range(1, MEMBERS)]
    along = [lax.rem(me + k, MEMBERS) for k in range(2, MEMBERS, 2)]
    beside = me + 1 - 2 * lax.rem(me, 2)
    crossed = [lax.rem(beside + k, MEMBERS) for k in range(0, MEMBERS, 2)]

    own_idx = pltpu.make_async_copy(send_ref.at[0, me], idx_ref.at[0], idx_sem.at[0])
    own_idx.start()
    own_smem = pltpu.make_async_copy(send_ref.at[0, me], idx_smem.at[0], idx_sem.at[1])
    own_smem.start()
    barrier = pltpu.get_barrier_semaphore()
    for other in others:
        pl.semaphore_signal(barrier, inc=1, device_id={"member": other}, device_id_type=MESH)
    pl.semaphore_signal(barrier, inc=1, device_id={"region": partner}, device_id_type=MESH)
    near = [(dz, dy) for dz in (-2, -1, 0, 1, 2) for dy in range(NY) if (dz, dy) != (0, 0)]
    for dz, dy in near:
        pl.semaphore_signal(
            barrier, inc=1, device_id={"region": region_at(z + dz, y + dy)}, device_id_type=MESH
        )
    own[...] = (obs_ref[...].astype(jnp.float32) / err_ref[...]).astype(jnp.bfloat16)
    dev2[0] = (innov2_ref[...] / err2_ref[...]).astype(jnp.bfloat16)
    pl.semaphore_wait(barrier, len(others) + 1 + len(near))

    def remote(src, dst, send, recv, where):
        return pltpu.make_async_remote_copy(
            src_ref=src, dst_ref=dst, send_sem=send, recv_sem=recv,
            device_id=where, device_id_type=MESH,
        )

    def pair_copy():
        return remote(own, pair, pair_send.at[0], pair_recv.at[0], {"region": partner})

    def pair_dev_copy():
        return remote(dev2.at[0], dev2.at[1], pair_send.at[1], pair_recv.at[1],
                      {"region": partner})

    def pair_idx_copy():
        return remote(send_ref.at[0, me], idx_ref.at[1], pair_send.at[2], pair_recv.at[2],
                      {"region": partner})

    def forward_copy(slot, owner):
        return remote(full.at[slot, owner], full.at[slot, owner], forward_send.at[slot, owner],
                      obs_recv.at[slot, owner], {"member": beside})

    def obs_copy(src, slot, owner, to):
        return remote(src, full.at[slot, owner], obs_send.at[slot, to], obs_recv.at[slot, owner],
                      {"member": to})

    def bg_copy(owner, to):
        cols = pl.ds(pl.multiple_of(to * columns, columns), columns)
        return remote(bg_ref.at[:, cols, :], raw.at[owner], bg_send.at[to], bg_recv.at[owner],
                      {"member": to})

    def block_copy(j, source, to):
        return remote(sent.at[j], pool.at[source], pool_send.at[j], pool_recv.at[source],
                      {"region": to})

    def block_dev_copy(j, source, to):
        return remote(sent_dev.at[j], pool_dev.at[source], dev_send.at[j], dev_recv.at[source],
                      {"region": to})

    def out_copy(g, owner, to):
        cols = pl.ds(g * OGROUP, OGROUP)
        return remote(result.at[to, cols], out_ref.at[owner, cols], out_send.at[g, to],
                      out_recv.at[g, owner], {"member": to})

    def spread(src, slot):
        for other in along + [beside]:
            obs_copy(src, slot, me, other).start()
        full[slot, me] = src[...]

    def forward(slot):
        for other in along:
            obs_copy(own, slot, other, other).wait_recv()
            forward_copy(slot, other).start()

    pair_copy().start()
    pair_dev_copy().start()
    pair_idx_copy().start()
    spread(own, 0)

    for c in range(columns):
        rho[pl.ds(c, 1), :] = taper_weights(taper_ref[pl.ds(c, 1), :], count_ref[c])

    def scatter(i, _):
        scatter_weights(2 * i, bidx_ref, rho, wmat)
        scatter_weights(2 * i + 1, bidx_ref, rho, wmat)
        return 0

    lax.fori_loop(0, columns // 2, scatter, 0)
    acc[...] = jnp.zeros_like(acc)

    forward(0)
    pair_copy().wait_recv()
    spread(pair, 1)
    own_idx.wait()
    own_smem.wait()

    def build(slot):
        for other in crossed:
            obs_copy(own, slot, other, other).wait_recv()
        for q in range(obs_count // SLOT):
            part = full[slot, :, :, q * SLOT : (q + 1) * SLOT]
            part = part.reshape(K, SLOT).astype(jnp.float32)
            table[pl.ds(slot * obs_count + q * SLOT, SLOT), :] = part.T

    def gather(slot, to):
        start = slot * obs_count
        parts = []
        for h in range(SLOT // LANES):
            rows = [
                table[pl.ds(idx_smem[slot, to, h * LANES + j] + start, 1), :] for j in range(LANES)
            ]
            parts.append(jnp.concatenate(rows, axis=0).T.astype(jnp.bfloat16))
        picked = dev_pick(idx_ref[slot, pl.ds(to, 1), :], dev2[slot])
        return jnp.concatenate(parts, axis=1), picked

    def send(j, _):
        slot, dz, dy = place(j)
        to = region_at(z + dz, y + dy)
        source = region_at(z + 4 * slot, y)
        block, dev = gather(slot, to)
        sent[j] = block
        sent_dev[j] = dev
        block_copy(j, source, to).start()
        block_dev_copy(j, source, to).start()
        return 0

    build(0)
    lax.fori_loop(0, 8, send, 0)
    forward(1)
    lax.fori_loop(8, 16, send, 0)
    pair_dev_copy().wait_recv()
    pair_idx_copy().wait_recv()
    pair_smem = pltpu.make_async_copy(idx_ref.at[1], idx_smem.at[1], idx_sem.at[0])
    pair_smem.start()
    for other in others:
        bg_copy(me, other).start()
    own_cols = pl.ds(pl.multiple_of(me * columns, columns), columns)
    keep_bg = pltpu.make_async_copy(bg_ref.at[:, own_cols, :], raw.at[me], bg_send.at[me])
    keep_bg.start()
    build(1)
    pair_smem.wait()
    lax.fori_loop(16, BLOCKS, send, 0)

    def local(slot, _):
        source = region_at(z + 4 * slot, y)
        block, dev = gather(slot, region)
        pool[source] = block
        pool_dev[source] = dev
        return 0

    lax.fori_loop(0, 2, local, 0)

    def add(sources):
        parts = [(source, pool[source], pool_dev[source]) for source in sources]
        gram_blocks(parts, wmat, right, acc)

    add([region, partner])

    def receive(i, _):
        sources = []
        for j in (2 * i, 2 * i + 1):
            slot, dz, dy = place(j)
            source = region_at(z - dz + 4 * slot, y - dy)
            block_copy(j, source, region).wait_recv()
            block_dev_copy(j, source, region).wait_recv()
            sources.append(source)
        add(sources)
        return 0

    lax.fori_loop(0, 8, receive, 0)
    keep_bg.wait()
    for other in others:
        bg_copy(other, other).wait_recv()
    permute_state(raw, state)
    lax.fori_loop(8, BLOCKS // 2, receive, 0)

    def own_out(g):
        cols = pl.ds(g * OGROUP, OGROUP)
        return pltpu.make_async_copy(result.at[me, cols], out_ref.at[me, cols], out_send.at[g, me])

    def group(i, _):
        first = i * CGROUP
        where = [pl.ds(pl.multiple_of((first + k) * K, K), K) for k in range(CGROUP)]
        grams = [acc[0:K, w] for w in where]
        shifts = [acc[K : K + 16, w] for w in where]
        done = transforms(grams, shifts)
        for h in range(CGROUP // OGROUP):
            g = i * (CGROUP // OGROUP) + h
            for k in range(OGROUP):
                at = h * OGROUP + k
                analyse(first + at, done[at], state, result)
            for other in others:
                out_copy(g, me, other).start()
            own_out(g).start()
        return 0

    groups = columns // OGROUP
    lax.fori_loop(0, columns // CGROUP, group, 0)

    pair_copy().wait_send()
    pair_dev_copy().wait_send()
    pair_idx_copy().wait_send()
    for other in along + [beside]:
        obs_copy(own, 0, me, other).wait_send()
        obs_copy(pair, 1, me, other).wait_send()
    for other in along:
        forward_copy(0, other).wait_send()
        forward_copy(1, other).wait_send()
    for other in others:
        bg_copy(me, other).wait_send()

    def drain(j, _):
        block_copy(j, region, region).wait_send()
        block_dev_copy(j, region, region).wait_send()
        return 0

    lax.fori_loop(0, BLOCKS, drain, 0)

    def finish(g, _):
        for other in others:
            out_copy(g, me, other).wait_send()
            out_copy(g, other, other).wait_recv()
        own_out(g).wait()
        return 0

    lax.fori_loop(0, groups, finish, 0)


def assimilate(send_index, obs_anom, innovation, obs_error, block_rows, taper_index, block_count,
               background):
    columns, places = block_rows.shape
    own, obs_count = obs_anom.shape
    values = background.shape[2]
    groups = columns // OGROUP
    bf16, f32 = jnp.bfloat16, jnp.float32
    dma = pltpu.SemaphoreType.DMA
    anywhere = pl.BlockSpec(memory_space=pl.ANY)
    return pl.pallas_call(
        kernel,
        out_shape=jax.ShapeDtypeStruct((MEMBERS, columns, own, values), bf16),
        in_specs=[anywhere] + [VMEM_SPEC] * 6 + [SMEM_SPEC, anywhere],
        out_specs=anywhere,
        scratch_shapes=[
            pltpu.SMEM((2, REGIONS, SLOT), jnp.int32),
            pltpu.VMEM((2, REGIONS, SLOT), jnp.int32),
            pltpu.VMEM((own, obs_count), bf16),
            pltpu.VMEM((2, MEMBERS, own, obs_count), bf16),
            pltpu.VMEM((own, obs_count), bf16),
            pltpu.VMEM((2, obs_count // LANES, LANES), bf16),
            pltpu.VMEM((2 * obs_count, K), f32),
            pltpu.VMEM((BLOCKS, K, SLOT), bf16),
            pltpu.VMEM((BLOCKS, 1, SLOT), f32),
            pltpu.VMEM((REGIONS, K, SLOT), bf16),
            pltpu.VMEM((REGIONS, 1, SLOT), f32),
            pltpu.VMEM((MEMBERS, own, columns, values), bf16),
            pltpu.VMEM((MEMBERS, columns, own, values), bf16),
            pltpu.VMEM((MEMBERS, columns, own, values), bf16),
            pltpu.VMEM((columns, LANES, LANES), f32),
            pltpu.VMEM((columns, places), f32),
            pltpu.VMEM((K + 16, 2 * SLOT), bf16),
            pltpu.VMEM((K + 16, columns * K), f32),
            dma((2,)),
            dma((2, MEMBERS)),
            dma((2, MEMBERS)),
            dma((2, MEMBERS)),
            dma((3,)),
            dma((3,)),
            dma((MEMBERS,)),
            dma((MEMBERS,)),
            dma((BLOCKS,)),
            dma((REGIONS,)),
            dma((BLOCKS,)),
            dma((REGIONS,)),
            dma((groups, MEMBERS)),
            dma((groups, MEMBERS)),
        ],
        compiler_params=pltpu.CompilerParams(
            vmem_limit_bytes=56 * 2**20, collective_id=0, has_side_effects=True
        ),
        cost_estimate=pl.CostEstimate(
            flops=2 * 10**10, bytes_accessed=12 * 2**20, transcendentals=0
        ),
    )(
        send_index,
        obs_anom,
        obs_error.reshape(1, obs_count),
        innovation.reshape(-1, LANES),
        obs_error.reshape(-1, LANES),
        block_rows,
        taper_index,
        block_count,
        background,
    )


def shards(
    background, obs_anom, innovation, obs_error, send_index, block_index, block_count, taper_index
):
    own, columns_all, values = background.shape
    result = assimilate(
        send_index, obs_anom, innovation, obs_error, block_index[0, 0], taper_index[0, 0],
        block_count[0, 0], background,
    )
    return result.reshape(columns_all, own, values).transpose(1, 0, 2)


def solution(mesh):
    in_specs = (
        P("member", "region", None),
        P("member", "region"),
        P("region"),
        P("region"),
        P("region", None, None, None),
        P("region", "member", None, None),
        P("region", "member", None),
        P("region", "member", None, None),
    )
    out_specs = P("member", "region", None)
    return jax.shard_map(shards, mesh=mesh, in_specs=in_specs, out_specs=out_specs, check_vma=False)
```

```python
import jax
import jax.numpy as jnp
from jax import lax
from jax.experimental import pallas as pl
from jax.experimental.pallas import tpu as pltpu
from jax.sharding import PartitionSpec as P

K = 128
SLOT = 512
NTAPER = 64
NS_ITERS = 6
LANES = 128
CGROUP = 4
OGROUP = 4
RESTORE_STEPS = 4
MEMBERS = 8
REGIONS = 32
NZ = 8
NY = 4
BLOCKS = 30
MESH = pl.DeviceIdType.MESH

NT = (((1,), (1,)), ((), ()))
VMEM_SPEC = pl.BlockSpec(memory_space=pltpu.VMEM)
SMEM_SPEC = pl.BlockSpec(memory_space=pltpu.SMEM)


def taper_weights(taper_index, block_count):
    radius = 2.0 * (taper_index.astype(jnp.float32) + 0.5) / NTAPER
    r2 = radius * radius
    r3 = r2 * radius
    r4 = r2 * r2
    r5 = r4 * radius
    inside_part = 1.0 - 5.0 / 3.0 * r2 + 0.625 * r3 + 0.5 * r4 - 0.25 * r5
    outside_part = (
        4.0 - 5.0 * radius + 5.0 / 3.0 * r2 + 0.625 * r3 - 0.5 * r4 + r5 / 12.0
        - 2.0 / (3.0 * radius)
    )
    weight = jnp.maximum(jnp.where(radius < 1.0, inside_part, outside_part), 0.0)
    places = lax.broadcasted_iota(jnp.int32, taper_index.shape, 1)
    return jnp.where(places < block_count, weight, 0.0)


def dev_pick(idx, dscaled):
    low = lax.broadcasted_iota(jnp.int32, (LANES, SLOT), 0) == (idx & (LANES - 1))
    picked = jnp.dot(
        dscaled, low.astype(jnp.float32).astype(jnp.bfloat16), preferred_element_type=jnp.float32
    )
    high = lax.broadcasted_iota(jnp.int32, picked.shape, 0) == (idx >> 7)
    return jnp.sum(jnp.where(high, picked, 0.0), axis=0, keepdims=True)


def split(x):
    high = x.astype(jnp.bfloat16)
    low = (x - high.astype(jnp.float32)).astype(jnp.bfloat16)
    return high, low


def dot3(a, b):
    ah, al = a
    bh, bl = b
    return jnp.dot(
        jnp.concatenate([ah, al, ah], axis=1),
        jnp.concatenate([bh, bh, bl], axis=0),
        preferred_element_type=jnp.float32,
    )


def scatter_weights(c, bidx_ref, rho, wmat):
    p = bidx_ref[pl.ds(c, 1), :]
    weight = rho[pl.ds(c, 1), :]
    count = p.shape[1]
    rows = lax.broadcasted_iota(jnp.int32, (LANES, count), 0)
    first = (rows == (p >> 7)).astype(jnp.float32).astype(jnp.bfloat16)
    high = weight.astype(jnp.bfloat16).astype(jnp.float32)
    hit = rows == (p & (LANES - 1))
    second = jnp.concatenate(
        [
            jnp.where(hit, high, 0.0).astype(jnp.bfloat16),
            jnp.where(hit, weight - high, 0.0).astype(jnp.bfloat16),
        ],
        axis=0,
    )
    both = lax.dot_general(first, second, NT, preferred_element_type=jnp.float32)
    wmat[c] = both[:, :LANES] + both[:, LANES:]


def gram_blocks(parts, wmat, right, acc):
    columns = wmat.shape[0]
    lead = SLOT // LANES
    first = lax.broadcasted_iota(jnp.int32, (16, SLOT), 0) == 0
    values = []
    for b, (r, block, dev) in enumerate(parts):
        lanes = slice(b * SLOT, (b + 1) * SLOT)
        right[0:K, lanes] = block
        right[K : K + 16, lanes] = jnp.where(first, dev, 0.0).astype(jnp.bfloat16)
        values.append(block.astype(jnp.float32))
    for c in range(0, columns, 2):
        weighted = []
        for column in (c, c + 1):
            pieces = []
            for v, (r, block, dev) in zip(values, parts):
                for q in range(lead):
                    w = wmat[column, pl.ds(r * lead + q, 1), :]
                    pieces.append((v[:, q * LANES : (q + 1) * LANES] * w).astype(jnp.bfloat16))
            weighted.append(jnp.concatenate(pieces, axis=1))
        acc[:, c * K : (c + 2) * K] += lax.dot_general(
            right[...], jnp.concatenate(weighted, axis=0), NT, preferred_element_type=jnp.float32
        )


def eye():
    shape = (K, K)
    same = lax.broadcasted_iota(jnp.int32, shape, 0) == lax.broadcasted_iota(jnp.int32, shape, 1)
    return same.astype(jnp.float32)


def transforms(grams, shifts):
    identity = eye()
    members = float(K)
    mats = [g + (members - 1.0) * identity for g in grams]
    norms = [jnp.sqrt(jnp.sum(m * m, axis=(0, 1), keepdims=True)) for m in mats]
    ys = [m / n for m, n in zip(mats, norms)]
    zs = [1.5 * identity - 0.5 * y for y in ys]
    ys = [dot3(split(z), split(y)) for z, y in zip(zs, ys)]
    for sweep in range(1, NS_ITERS):
        sy = [split(y) for y in ys]
        sz = [split(z) for z in zs]
        sf = [split(1.5 * identity - 0.5 * dot3(z, y)) for z, y in zip(sz, sy)]
        if sweep == NS_ITERS - 1:
            zs = [dot3(f, z) for f, z in zip(sf, sz)]
        else:
            both = [
                dot3(f, tuple(jnp.concatenate([a, b], axis=1) for a, b in zip(y, z)))
                for f, y, z in zip(sf, sy, sz)
            ]
            ys = [b[:, :K] for b in both]
            zs = [b[:, K:] for b in both]
    sz = [split(z) for z in zs]
    half = [dot3(split(p), z) for z, p in zip(sz, shifts)]
    full = [dot3(split(h), z) for z, h in zip(sz, half)]
    out = []
    for z, f, n in zip(zs, full, norms):
        out.append(jnp.sqrt(members - 1.0) * z / jnp.sqrt(n) + f[0:1, :] / n)
    return out


def analyse(c, transform, bg_ref, out_ref):
    state = bg_ref[:, c].reshape(K, bg_ref.shape[3]).astype(jnp.float32)
    mean_state = jnp.sum(state, axis=0, keepdims=True) * (1.0 / K)
    anomalies = (state - mean_state).astype(jnp.bfloat16)
    combined = jnp.dot(
        transform.astype(jnp.bfloat16), anomalies, preferred_element_type=jnp.float32
    )
    result = (mean_state + combined).astype(jnp.bfloat16)
    out_ref[:, c] = result.reshape(out_ref.shape[0], out_ref.shape[2], out_ref.shape[3])


def place(j):
    block = j + 2 * (j // 24)
    combo, dy = 2 * (block // 8) + block % 2, (block // 2) % 4
    distance = 2 - (combo + 2) // 4
    dz = distance * (1 - 2 * (combo % 2))
    slot = combo // 4 - combo // 7
    return slot, dz, dy


def region_at(z, y):
    return ((z + 16) % NZ) * NY + (y + 8) % NY


def swap_matrix(count):
    a = lax.broadcasted_iota(jnp.int32, (count, count), 0)
    b = lax.broadcasted_iota(jnp.int32, (count, count), 1)
    swap = (a // 16 == b % 16) & (a % 16 == b // 16)
    return swap.astype(jnp.float32).astype(jnp.bfloat16)


def swap_block(swap, block):
    rows = block.reshape(swap.shape[0], block.shape[2])
    moved = jnp.dot(swap, rows, preferred_element_type=jnp.float32).astype(jnp.bfloat16)
    return moved.reshape(block.shape)


def permute_state(raw, state):
    swap = swap_matrix(raw.shape[1] * raw.shape[2])
    for m in range(raw.shape[0]):
        state[m] = swap_block(swap, raw[m])


def restore_kernel(blocks_ref, out_ref):
    columns, own = blocks_ref.shape[1:3]
    swap = swap_matrix(columns * own)
    for m in range(blocks_ref.shape[0]):
        out_ref[:, m * columns : (m + 1) * columns, :] = swap_block(swap, blocks_ref[m])


def restore(blocks):
    members, columns, own, values = blocks.shape
    step = members // RESTORE_STEPS
    return pl.pallas_call(
        restore_kernel,
        grid=(RESTORE_STEPS,),
        out_shape=jax.ShapeDtypeStruct((own, members * columns, values), blocks.dtype),
        in_specs=[pl.BlockSpec((step, columns, own, values), lambda i: (i, 0, 0, 0))],
        out_specs=pl.BlockSpec((own, step * columns, values), lambda i: (0, i, 0)),
        compiler_params=pltpu.CompilerParams(vmem_limit_bytes=60 * 2**20),
    )(blocks)


def kernel(send_ref, obs_ref, err_ref, innov2_ref, err2_ref, bidx_ref, taper_ref,
           count_ref, bg_ref, out_ref,
           idx_smem, idx_ref, own, full, pair, dev2, table, sent, sent_dev, pool, pool_dev,
           raw, state, result, wmat, rho, right, acc,
           idx_sem, obs_send, obs_recv, forward_send, pair_send, pair_recv, bg_send, bg_recv,
           pool_send, pool_recv, dev_send, dev_recv, out_send, out_recv):
    me = lax.axis_index("member")
    region = lax.axis_index("region")
    z, y = region // NY, region % NY
    partner = region_at(z + 4, y)
    columns = bidx_ref.shape[0]
    obs_count = obs_ref.shape[1]
    others = [lax.rem(me + k, MEMBERS) for k in range(1, MEMBERS)]
    along = [lax.rem(me + k, MEMBERS) for k in range(2, MEMBERS, 2)]
    beside = me + 1 - 2 * lax.rem(me, 2)
    crossed = [lax.rem(beside + k, MEMBERS) for k in range(0, MEMBERS, 2)]

    own_idx = pltpu.make_async_copy(send_ref.at[0, me], idx_ref.at[0], idx_sem.at[0])
    own_idx.start()
    own_smem = pltpu.make_async_copy(send_ref.at[0, me], idx_smem.at[0], idx_sem.at[1])
    own_smem.start()
    barrier = pltpu.get_barrier_semaphore()
    for other in others:
        pl.semaphore_signal(barrier, inc=1, device_id={"member": other}, device_id_type=MESH)
    pl.semaphore_signal(barrier, inc=1, device_id={"region": partner}, device_id_type=MESH)
    near = [(dz, dy) for dz in (-2, -1, 0, 1, 2) for dy in range(NY) if (dz, dy) != (0, 0)]
    for dz, dy in near:
        pl.semaphore_signal(
            barrier, inc=1, device_id={"region": region_at(z + dz, y + dy)}, device_id_type=MESH
        )
    own[...] = (obs_ref[...].astype(jnp.float32) / err_ref[...]).astype(jnp.bfloat16)
    dev2[0] = (innov2_ref[...] / err2_ref[...]).astype(jnp.bfloat16)
    pl.semaphore_wait(barrier, len(others) + 1 + len(near))

    def remote(src, dst, send, recv, where):
        return pltpu.make_async_remote_copy(
            src_ref=src, dst_ref=dst, send_sem=send, recv_sem=recv,
            device_id=where, device_id_type=MESH,
        )

    def pair_copy():
        return remote(own, pair, pair_send.at[0], pair_recv.at[0], {"region": partner})

    def pair_dev_copy():
        return remote(dev2.at[0], dev2.at[1], pair_send.at[1], pair_recv.at[1],
                      {"region": partner})

    def pair_idx_copy():
        return remote(send_ref.at[0, me], idx_ref.at[1], pair_send.at[2], pair_recv.at[2],
                      {"region": partner})

    def forward_copy(slot, owner):
        return remote(full.at[slot, owner], full.at[slot, owner], forward_send.at[slot, owner],
                      obs_recv.at[slot, owner], {"member": beside})

    def obs_copy(src, slot, owner, to):
        return remote(src, full.at[slot, owner], obs_send.at[slot, to], obs_recv.at[slot, owner],
                      {"member": to})

    def bg_copy(owner, to):
        cols = pl.ds(pl.multiple_of(to * columns, columns), columns)
        return remote(bg_ref.at[:, cols, :], raw.at[owner], bg_send.at[to], bg_recv.at[owner],
                      {"member": to})

    def block_copy(j, source, to):
        return remote(sent.at[j], pool.at[source], pool_send.at[j], pool_recv.at[source],
                      {"region": to})

    def block_dev_copy(j, source, to):
        return remote(sent_dev.at[j], pool_dev.at[source], dev_send.at[j], dev_recv.at[source],
                      {"region": to})

    def out_copy(g, owner, to):
        cols = pl.ds(g * OGROUP, OGROUP)
        return remote(result.at[to, cols], out_ref.at[owner, cols], out_send.at[g, to],
                      out_recv.at[g, owner], {"member": to})

    def spread(src, slot):
        for other in along + [beside]:
            obs_copy(src, slot, me, other).start()
        full[slot, me] = src[...]

    def forward(slot):
        for other in along:
            obs_copy(own, slot, other, other).wait_recv()
            forward_copy(slot, other).start()

    pair_copy().start()
    pair_dev_copy().start()
    pair_idx_copy().start()
    spread(own, 0)

    for c in range(columns):
        rho[pl.ds(c, 1), :] = taper_weights(taper_ref[pl.ds(c, 1), :], count_ref[c])

    def scatter(i, _):
        scatter_weights(2 * i, bidx_ref, rho, wmat)
        scatter_weights(2 * i + 1, bidx_ref, rho, wmat)
        return 0

    lax.fori_loop(0, columns // 2, scatter, 0)
    acc[...] = jnp.zeros_like(acc)

    forward(0)
    pair_copy().wait_recv()
    spread(pair, 1)
    own_idx.wait()
    own_smem.wait()

    def build(slot):
        for other in crossed:
            obs_copy(own, slot, other, other).wait_recv()
        for q in range(obs_count // SLOT):
            part = full[slot, :, :, q * SLOT : (q + 1) * SLOT]
            part = part.reshape(K, SLOT).astype(jnp.float32)
            table[pl.ds(slot * obs_count + q * SLOT, SLOT), :] = part.T

    def gather(slot, to):
        start = slot * obs_count
        parts = []
        for h in range(SLOT // LANES):
            rows = [
                table[pl.ds(idx_smem[slot, to, h * LANES + j] + start, 1), :] for j in range(LANES)
            ]
            parts.append(jnp.concatenate(rows, axis=0).T.astype(jnp.bfloat16))
        picked = dev_pick(idx_ref[slot, pl.ds(to, 1), :], dev2[slot])
        return jnp.concatenate(parts, axis=1), picked

    def send(j, _):
        slot, dz, dy = place(j)
        to = region_at(z + dz, y + dy)
        source = region_at(z + 4 * slot, y)
        block, dev = gather(slot, to)
        sent[j] = block
        sent_dev[j] = dev
        block_copy(j, source, to).start()
        block_dev_copy(j, source, to).start()
        return 0

    build(0)
    lax.fori_loop(0, 8, send, 0)
    forward(1)
    lax.fori_loop(8, 16, send, 0)
    pair_dev_copy().wait_recv()
    pair_idx_copy().wait_recv()
    pair_smem = pltpu.make_async_copy(idx_ref.at[1], idx_smem.at[1], idx_sem.at[0])
    pair_smem.start()
    for other in others:
        bg_copy(me, other).start()
    own_cols = pl.ds(pl.multiple_of(me * columns, columns), columns)
    keep_bg = pltpu.make_async_copy(bg_ref.at[:, own_cols, :], raw.at[me], bg_send.at[me])
    keep_bg.start()
    build(1)
    pair_smem.wait()
    lax.fori_loop(16, BLOCKS, send, 0)

    def local(slot, _):
        source = region_at(z + 4 * slot, y)
        block, dev = gather(slot, region)
        pool[source] = block
        pool_dev[source] = dev
        return 0

    lax.fori_loop(0, 2, local, 0)

    def add(sources):
        parts = [(source, pool[source], pool_dev[source]) for source in sources]
        gram_blocks(parts, wmat, right, acc)

    add([region, partner])

    def receive(i, _):
        sources = []
        for j in (2 * i, 2 * i + 1):
            slot, dz, dy = place(j)
            source = region_at(z - dz + 4 * slot, y - dy)
            block_copy(j, source, region).wait_recv()
            block_dev_copy(j, source, region).wait_recv()
            sources.append(source)
        add(sources)
        return 0

    lax.fori_loop(0, 8, receive, 0)
    keep_bg.wait()
    for other in others:
        bg_copy(other, other).wait_recv()
    permute_state(raw, state)
    lax.fori_loop(8, BLOCKS // 2, receive, 0)

    def own_out(g):
        cols = pl.ds(g * OGROUP, OGROUP)
        return pltpu.make_async_copy(result.at[me, cols], out_ref.at[me, cols], out_send.at[g, me])

    def group(i, _):
        first = i * CGROUP
        where = [pl.ds(pl.multiple_of((first + k) * K, K), K) for k in range(CGROUP)]
        grams = [acc[0:K, w] for w in where]
        shifts = [acc[K : K + 16, w] for w in where]
        done = transforms(grams, shifts)
        for h in range(CGROUP // OGROUP):
            g = i * (CGROUP // OGROUP) + h
            for k in range(OGROUP):
                at = h * OGROUP + k
                analyse(first + at, done[at], state, result)
            for other in others:
                out_copy(g, me, other).start()
            own_out(g).start()
        return 0

    groups = columns // OGROUP
    lax.fori_loop(0, columns // CGROUP, group, 0)

    pair_copy().wait_send()
    pair_dev_copy().wait_send()
    pair_idx_copy().wait_send()
    for other in along + [beside]:
        obs_copy(own, 0, me, other).wait_send()
        obs_copy(pair, 1, me, other).wait_send()
    for other in along:
        forward_copy(0, other).wait_send()
        forward_copy(1, other).wait_send()
    for other in others:
        bg_copy(me, other).wait_send()

    def drain(j, _):
        block_copy(j, region, region).wait_send()
        block_dev_copy(j, region, region).wait_send()
        return 0

    lax.fori_loop(0, BLOCKS, drain, 0)

    def finish(g, _):
        for other in others:
            out_copy(g, me, other).wait_send()
            out_copy(g, other, other).wait_recv()
        own_out(g).wait()
        return 0

    lax.fori_loop(0, groups, finish, 0)


def assimilate(send_index, obs_anom, innovation, obs_error, block_rows, taper_index, block_count,
               background):
    columns, places = block_rows.shape
    own, obs_count = obs_anom.shape
    values = background.shape[2]
    groups = columns // OGROUP
    bf16, f32 = jnp.bfloat16, jnp.float32
    dma = pltpu.SemaphoreType.DMA
    anywhere = pl.BlockSpec(memory_space=pl.ANY)
    return pl.pallas_call(
        kernel,
        out_shape=jax.ShapeDtypeStruct((MEMBERS, columns, own, values), bf16),
        in_specs=[anywhere] + [VMEM_SPEC] * 6 + [SMEM_SPEC, anywhere],
        out_specs=anywhere,
        scratch_shapes=[
            pltpu.SMEM((2, REGIONS, SLOT), jnp.int32),
            pltpu.VMEM((2, REGIONS, SLOT), jnp.int32),
            pltpu.VMEM((own, obs_count), bf16),
            pltpu.VMEM((2, MEMBERS, own, obs_count), bf16),
            pltpu.VMEM((own, obs_count), bf16),
            pltpu.VMEM((2, obs_count // LANES, LANES), bf16),
            pltpu.VMEM((2 * obs_count, K), f32),
            pltpu.VMEM((BLOCKS, K, SLOT), bf16),
            pltpu.VMEM((BLOCKS, 1, SLOT), f32),
            pltpu.VMEM((REGIONS, K, SLOT), bf16),
            pltpu.VMEM((REGIONS, 1, SLOT), f32),
            pltpu.VMEM((MEMBERS, own, columns, values), bf16),
            pltpu.VMEM((MEMBERS, columns, own, values), bf16),
            pltpu.VMEM((MEMBERS, columns, own, values), bf16),
            pltpu.VMEM((columns, LANES, LANES), f32),
            pltpu.VMEM((columns, places), f32),
            pltpu.VMEM((K + 16, 2 * SLOT), bf16),
            pltpu.VMEM((K + 16, columns * K), f32),
            dma((2,)),
            dma((2, MEMBERS)),
            dma((2, MEMBERS)),
            dma((2, MEMBERS)),
            dma((3,)),
            dma((3,)),
            dma((MEMBERS,)),
            dma((MEMBERS,)),
            dma((BLOCKS,)),
            dma((REGIONS,)),
            dma((BLOCKS,)),
            dma((REGIONS,)),
            dma((groups, MEMBERS)),
            dma((groups, MEMBERS)),
        ],
        compiler_params=pltpu.CompilerParams(
            vmem_limit_bytes=56 * 2**20, collective_id=0, has_side_effects=True
        ),
        cost_estimate=pl.CostEstimate(
            flops=2 * 10**10, bytes_accessed=12 * 2**20, transcendentals=0
        ),
    )(
        send_index,
        obs_anom,
        obs_error.reshape(1, obs_count),
        innovation.reshape(-1, LANES),
        obs_error.reshape(-1, LANES),
        block_rows,
        taper_index,
        block_count,
        background,
    )


def shards(
    background, obs_anom, innovation, obs_error, send_index, block_index, block_count, taper_index
):
    result = assimilate(
        send_index, obs_anom, innovation, obs_error, block_index[0, 0], taper_index[0, 0],
        block_count[0, 0], background,
    )
    return restore(result)


def solution(mesh):
    in_specs = (
        P("member", "region", None),
        P("member", "region"),
        P("region"),
        P("region"),
        P("region", None, None, None),
        P("region", "member", None, None),
        P("region", "member", None),
        P("region", "member", None, None),
    )
    out_specs = P("member", "region", None)
    return jax.shard_map(shards, mesh=mesh, in_specs=in_specs, out_specs=out_specs, check_vma=False)
```

```python
import jax
import jax.numpy as jnp
from jax import lax
from jax.experimental import pallas as pl
from jax.experimental.pallas import tpu as pltpu
from jax.sharding import PartitionSpec as P

K = 128
SLOT = 512
NTAPER = 64
NS_ITERS = 6
LANES = 128
CGROUP = 4
OGROUP = 4
RESTORE_STEPS = 2
MEMBERS = 8
REGIONS = 32
NZ = 8
NY = 4
BLOCKS = 30
MESH = pl.DeviceIdType.MESH

NT = (((1,), (1,)), ((), ()))
VMEM_SPEC = pl.BlockSpec(memory_space=pltpu.VMEM)
SMEM_SPEC = pl.BlockSpec(memory_space=pltpu.SMEM)


def taper_weights(taper_index, block_count):
    radius = 2.0 * (taper_index.astype(jnp.float32) + 0.5) / NTAPER
    r2 = radius * radius
    r3 = r2 * radius
    r4 = r2 * r2
    r5 = r4 * radius
    inside_part = 1.0 - 5.0 / 3.0 * r2 + 0.625 * r3 + 0.5 * r4 - 0.25 * r5
    outside_part = (
        4.0 - 5.0 * radius + 5.0 / 3.0 * r2 + 0.625 * r3 - 0.5 * r4 + r5 / 12.0
        - 2.0 / (3.0 * radius)
    )
    weight = jnp.maximum(jnp.where(radius < 1.0, inside_part, outside_part), 0.0)
    places = lax.broadcasted_iota(jnp.int32, taper_index.shape, 1)
    return jnp.where(places < block_count, weight, 0.0)


def dev_pick(idx, dscaled):
    low = lax.broadcasted_iota(jnp.int32, (LANES, SLOT), 0) == (idx & (LANES - 1))
    picked = jnp.dot(
        dscaled, low.astype(jnp.float32).astype(jnp.bfloat16), preferred_element_type=jnp.float32
    )
    high = lax.broadcasted_iota(jnp.int32, picked.shape, 0) == (idx >> 7)
    return jnp.sum(jnp.where(high, picked, 0.0), axis=0, keepdims=True)


def split(x):
    high = x.astype(jnp.bfloat16)
    low = (x - high.astype(jnp.float32)).astype(jnp.bfloat16)
    return high, low


def dot3(a, b):
    ah, al = a
    bh, bl = b
    return jnp.dot(
        jnp.concatenate([ah, al, ah], axis=1),
        jnp.concatenate([bh, bh, bl], axis=0),
        preferred_element_type=jnp.float32,
    )


def scatter_weights(c, bidx_ref, rho, wmat):
    p = bidx_ref[pl.ds(c, 1), :]
    weight = rho[pl.ds(c, 1), :]
    count = p.shape[1]
    rows = lax.broadcasted_iota(jnp.int32, (LANES, count), 0)
    first = (rows == (p >> 7)).astype(jnp.float32).astype(jnp.bfloat16)
    high = weight.astype(jnp.bfloat16).astype(jnp.float32)
    hit = rows == (p & (LANES - 1))
    second = jnp.concatenate(
        [
            jnp.where(hit, high, 0.0).astype(jnp.bfloat16),
            jnp.where(hit, weight - high, 0.0).astype(jnp.bfloat16),
        ],
        axis=0,
    )
    both = lax.dot_general(first, second, NT, preferred_element_type=jnp.float32)
    wmat[c] = both[:, :LANES] + both[:, LANES:]


def gram_blocks(parts, wmat, right, acc):
    columns = wmat.shape[0]
    lead = SLOT // LANES
    first = lax.broadcasted_iota(jnp.int32, (16, SLOT), 0) == 0
    values = []
    for b, (r, block, dev) in enumerate(parts):
        lanes = slice(b * SLOT, (b + 1) * SLOT)
        right[0:K, lanes] = block
        right[K : K + 16, lanes] = jnp.where(first, dev, 0.0).astype(jnp.bfloat16)
        values.append(block.astype(jnp.float32))
    for c in range(0, columns, 2):
        weighted = []
        for column in (c, c + 1):
            pieces = []
            for v, (r, block, dev) in zip(values, parts):
                for q in range(lead):
                    w = wmat[column, pl.ds(r * lead + q, 1), :]
                    pieces.append((v[:, q * LANES : (q + 1) * LANES] * w).astype(jnp.bfloat16))
            weighted.append(jnp.concatenate(pieces, axis=1))
        acc[:, c * K : (c + 2) * K] += lax.dot_general(
            right[...], jnp.concatenate(weighted, axis=0), NT, preferred_element_type=jnp.float32
        )


def eye():
    shape = (K, K)
    same = lax.broadcasted_iota(jnp.int32, shape, 0) == lax.broadcasted_iota(jnp.int32, shape, 1)
    return same.astype(jnp.float32)


def transforms(grams, shifts):
    identity = eye()
    members = float(K)
    mats = [g + (members - 1.0) * identity for g in grams]
    norms = [jnp.sqrt(jnp.sum(m * m, axis=(0, 1), keepdims=True)) for m in mats]
    ys = [m / n for m, n in zip(mats, norms)]
    zs = [1.5 * identity - 0.5 * y for y in ys]
    ys = [dot3(split(z), split(y)) for z, y in zip(zs, ys)]
    for sweep in range(1, NS_ITERS):
        sy = [split(y) for y in ys]
        sz = [split(z) for z in zs]
        sf = [split(1.5 * identity - 0.5 * dot3(z, y)) for z, y in zip(sz, sy)]
        if sweep == NS_ITERS - 1:
            zs = [dot3(f, z) for f, z in zip(sf, sz)]
        else:
            both = [
                dot3(f, tuple(jnp.concatenate([a, b], axis=1) for a, b in zip(y, z)))
                for f, y, z in zip(sf, sy, sz)
            ]
            ys = [b[:, :K] for b in both]
            zs = [b[:, K:] for b in both]
    sz = [split(z) for z in zs]
    half = [dot3(split(p), z) for z, p in zip(sz, shifts)]
    full = [dot3(split(h), z) for z, h in zip(sz, half)]
    out = []
    for z, f, n in zip(zs, full, norms):
        out.append(jnp.sqrt(members - 1.0) * z / jnp.sqrt(n) + f[0:1, :] / n)
    return out


def analyse(c, transform, bg_ref, out_ref):
    state = bg_ref[:, c].reshape(K, bg_ref.shape[3]).astype(jnp.float32)
    mean_state = jnp.sum(state, axis=0, keepdims=True) * (1.0 / K)
    anomalies = (state - mean_state).astype(jnp.bfloat16)
    combined = jnp.dot(
        transform.astype(jnp.bfloat16), anomalies, preferred_element_type=jnp.float32
    )
    result = (mean_state + combined).astype(jnp.bfloat16)
    out_ref[:, c] = result.reshape(out_ref.shape[0], out_ref.shape[2], out_ref.shape[3])


def place(j):
    block = j + 2 * (j // 24)
    combo, dy = 2 * (block // 8) + block % 2, (block // 2) % 4
    distance = 2 - (combo + 2) // 4
    dz = distance * (1 - 2 * (combo % 2))
    slot = combo // 4 - combo // 7
    return slot, dz, dy


def region_at(z, y):
    return ((z + 16) % NZ) * NY + (y + 8) % NY


def swap_matrix(count):
    a = lax.broadcasted_iota(jnp.int32, (count, count), 0)
    b = lax.broadcasted_iota(jnp.int32, (count, count), 1)
    swap = (a // 16 == b % 16) & (a % 16 == b // 16)
    return swap.astype(jnp.float32).astype(jnp.bfloat16)


def swap_block(swap, block):
    rows = block.reshape(swap.shape[0], block.shape[2])
    moved = jnp.dot(swap, rows, preferred_element_type=jnp.float32).astype(jnp.bfloat16)
    return moved.reshape(block.shape)


def permute_state(raw, state):
    swap = swap_matrix(raw.shape[1] * raw.shape[2])
    for m in range(raw.shape[0]):
        state[m] = swap_block(swap, raw[m])


def restore_kernel(blocks_ref, out_ref):
    columns, own = blocks_ref.shape[1:3]
    swap = swap_matrix(columns * own)
    for m in range(blocks_ref.shape[0]):
        out_ref[:, m * columns : (m + 1) * columns, :] = swap_block(swap, blocks_ref[m])


def restore(blocks):
    members, columns, own, values = blocks.shape
    step = members // RESTORE_STEPS
    return pl.pallas_call(
        restore_kernel,
        grid=(RESTORE_STEPS,),
        out_shape=jax.ShapeDtypeStruct((own, members * columns, values), blocks.dtype),
        in_specs=[pl.BlockSpec((step, columns, own, values), lambda i: (i, 0, 0, 0))],
        out_specs=pl.BlockSpec((own, step * columns, values), lambda i: (0, i, 0)),
        compiler_params=pltpu.CompilerParams(vmem_limit_bytes=60 * 2**20),
    )(blocks)


def kernel(send_ref, obs_ref, err_ref, innov2_ref, err2_ref, bidx_ref, taper_ref,
           count_ref, bg_ref, out_ref,
           idx_smem, idx_ref, own, full, pair, dev2, table, sent, sent_dev, pool, pool_dev,
           raw, state, result, wmat, rho, right, acc,
           idx_sem, obs_send, obs_recv, forward_send, pair_send, pair_recv, bg_send, bg_recv,
           pool_send, pool_recv, dev_send, dev_recv, out_send, out_recv):
    me = lax.axis_index("member")
    region = lax.axis_index("region")
    z, y = region // NY, region % NY
    partner = region_at(z + 4, y)
    columns = bidx_ref.shape[0]
    obs_count = obs_ref.shape[1]
    others = [lax.rem(me + k, MEMBERS) for k in range(1, MEMBERS)]
    along = [lax.rem(me + k, MEMBERS) for k in range(2, MEMBERS, 2)]
    beside = me + 1 - 2 * lax.rem(me, 2)
    crossed = [lax.rem(beside + k, MEMBERS) for k in range(0, MEMBERS, 2)]

    own_idx = pltpu.make_async_copy(send_ref.at[0, me], idx_ref.at[0], idx_sem.at[0])
    own_idx.start()
    own_smem = pltpu.make_async_copy(send_ref.at[0, me], idx_smem.at[0], idx_sem.at[1])
    own_smem.start()
    barrier = pltpu.get_barrier_semaphore()
    for other in others:
        pl.semaphore_signal(barrier, inc=1, device_id={"member": other}, device_id_type=MESH)
    pl.semaphore_signal(barrier, inc=1, device_id={"region": partner}, device_id_type=MESH)
    near = [(dz, dy) for dz in (-2, -1, 0, 1, 2) for dy in range(NY) if (dz, dy) != (0, 0)]
    for dz, dy in near:
        pl.semaphore_signal(
            barrier, inc=1, device_id={"region": region_at(z + dz, y + dy)}, device_id_type=MESH
        )
    own[...] = (obs_ref[...].astype(jnp.float32) / err_ref[...]).astype(jnp.bfloat16)
    dev2[0] = (innov2_ref[...] / err2_ref[...]).astype(jnp.bfloat16)
    pl.semaphore_wait(barrier, len(others) + 1 + len(near))

    def remote(src, dst, send, recv, where):
        return pltpu.make_async_remote_copy(
            src_ref=src, dst_ref=dst, send_sem=send, recv_sem=recv,
            device_id=where, device_id_type=MESH,
        )

    def pair_copy():
        return remote(own, pair, pair_send.at[0], pair_recv.at[0], {"region": partner})

    def pair_dev_copy():
        return remote(dev2.at[0], dev2.at[1], pair_send.at[1], pair_recv.at[1],
                      {"region": partner})

    def pair_idx_copy():
        return remote(send_ref.at[0, me], idx_ref.at[1], pair_send.at[2], pair_recv.at[2],
                      {"region": partner})

    def forward_copy(slot, owner):
        return remote(full.at[slot, owner], full.at[slot, owner], forward_send.at[slot, owner],
                      obs_recv.at[slot, owner], {"member": beside})

    def obs_copy(src, slot, owner, to):
        return remote(src, full.at[slot, owner], obs_send.at[slot, to], obs_recv.at[slot, owner],
                      {"member": to})

    def bg_copy(owner, to):
        cols = pl.ds(pl.multiple_of(to * columns, columns), columns)
        return remote(bg_ref.at[:, cols, :], raw.at[owner], bg_send.at[to], bg_recv.at[owner],
                      {"member": to})

    def block_copy(j, source, to):
        return remote(sent.at[j], pool.at[source], pool_send.at[j], pool_recv.at[source],
                      {"region": to})

    def block_dev_copy(j, source, to):
        return remote(sent_dev.at[j], pool_dev.at[source], dev_send.at[j], dev_recv.at[source],
                      {"region": to})

    def out_copy(g, owner, to):
        cols = pl.ds(g * OGROUP, OGROUP)
        return remote(result.at[to, cols], out_ref.at[owner, cols], out_send.at[g, to],
                      out_recv.at[g, owner], {"member": to})

    def spread(src, slot):
        for other in along + [beside]:
            obs_copy(src, slot, me, other).start()
        full[slot, me] = src[...]

    def forward(slot):
        for other in along:
            obs_copy(own, slot, other, other).wait_recv()
            forward_copy(slot, other).start()

    pair_copy().start()
    pair_dev_copy().start()
    pair_idx_copy().start()
    spread(own, 0)

    for c in range(columns):
        rho[pl.ds(c, 1), :] = taper_weights(taper_ref[pl.ds(c, 1), :], count_ref[c])

    def scatter(i, _):
        scatter_weights(2 * i, bidx_ref, rho, wmat)
        scatter_weights(2 * i + 1, bidx_ref, rho, wmat)
        return 0

    lax.fori_loop(0, columns // 2, scatter, 0)
    acc[...] = jnp.zeros_like(acc)

    forward(0)
    pair_copy().wait_recv()
    spread(pair, 1)
    own_idx.wait()
    own_smem.wait()

    def build(slot):
        for other in crossed:
            obs_copy(own, slot, other, other).wait_recv()
        for q in range(obs_count // SLOT):
            part = full[slot, :, :, q * SLOT : (q + 1) * SLOT]
            part = part.reshape(K, SLOT).astype(jnp.float32)
            table[pl.ds(slot * obs_count + q * SLOT, SLOT), :] = part.T

    def gather(slot, to):
        start = slot * obs_count
        parts = []
        for h in range(SLOT // LANES):
            rows = [
                table[pl.ds(idx_smem[slot, to, h * LANES + j] + start, 1), :] for j in range(LANES)
            ]
            parts.append(jnp.concatenate(rows, axis=0).T.astype(jnp.bfloat16))
        picked = dev_pick(idx_ref[slot, pl.ds(to, 1), :], dev2[slot])
        return jnp.concatenate(parts, axis=1), picked

    def send(j, _):
        slot, dz, dy = place(j)
        to = region_at(z + dz, y + dy)
        source = region_at(z + 4 * slot, y)
        block, dev = gather(slot, to)
        sent[j] = block
        sent_dev[j] = dev
        block_copy(j, source, to).start()
        block_dev_copy(j, source, to).start()
        return 0

    build(0)
    lax.fori_loop(0, 10, send, 0)
    forward(1)
    lax.fori_loop(10, 16, send, 0)
    pair_dev_copy().wait_recv()
    pair_idx_copy().wait_recv()
    pair_smem = pltpu.make_async_copy(idx_ref.at[1], idx_smem.at[1], idx_sem.at[0])
    pair_smem.start()
    for other in others:
        bg_copy(me, other).start()
    own_cols = pl.ds(pl.multiple_of(me * columns, columns), columns)
    keep_bg = pltpu.make_async_copy(bg_ref.at[:, own_cols, :], raw.at[me], bg_send.at[me])
    keep_bg.start()
    build(1)
    pair_smem.wait()
    lax.fori_loop(16, BLOCKS, send, 0)

    def local(slot, _):
        source = region_at(z + 4 * slot, y)
        block, dev = gather(slot, region)
        pool[source] = block
        pool_dev[source] = dev
        return 0

    lax.fori_loop(0, 2, local, 0)

    def add(sources):
        parts = [(source, pool[source], pool_dev[source]) for source in sources]
        gram_blocks(parts, wmat, right, acc)

    add([region, partner])

    def receive(i, _):
        sources = []
        for j in (2 * i, 2 * i + 1):
            slot, dz, dy = place(j)
            source = region_at(z - dz + 4 * slot, y - dy)
            block_copy(j, source, region).wait_recv()
            block_dev_copy(j, source, region).wait_recv()
            sources.append(source)
        add(sources)
        return 0

    lax.fori_loop(0, 8, receive, 0)
    keep_bg.wait()
    for other in others:
        bg_copy(other, other).wait_recv()
    permute_state(raw, state)
    lax.fori_loop(8, BLOCKS // 2, receive, 0)

    def own_out(g):
        cols = pl.ds(g * OGROUP, OGROUP)
        return pltpu.make_async_copy(result.at[me, cols], out_ref.at[me, cols], out_send.at[g, me])

    def group(i, _):
        first = i * CGROUP
        where = [pl.ds(pl.multiple_of((first + k) * K, K), K) for k in range(CGROUP)]
        grams = [acc[0:K, w] for w in where]
        shifts = [acc[K : K + 16, w] for w in where]
        done = transforms(grams, shifts)
        for h in range(CGROUP // OGROUP):
            g = i * (CGROUP // OGROUP) + h
            for k in range(OGROUP):
                at = h * OGROUP + k
                analyse(first + at, done[at], state, result)
            for other in others:
                out_copy(g, me, other).start()
            own_out(g).start()
        return 0

    groups = columns // OGROUP
    lax.fori_loop(0, columns // CGROUP, group, 0)

    pair_copy().wait_send()
    pair_dev_copy().wait_send()
    pair_idx_copy().wait_send()
    for other in along + [beside]:
        obs_copy(own, 0, me, other).wait_send()
        obs_copy(pair, 1, me, other).wait_send()
    for other in along:
        forward_copy(0, other).wait_send()
        forward_copy(1, other).wait_send()
    for other in others:
        bg_copy(me, other).wait_send()

    def drain(j, _):
        block_copy(j, region, region).wait_send()
        block_dev_copy(j, region, region).wait_send()
        return 0

    lax.fori_loop(0, BLOCKS, drain, 0)

    def finish(g, _):
        for other in others:
            out_copy(g, me, other).wait_send()
            out_copy(g, other, other).wait_recv()
        own_out(g).wait()
        return 0

    lax.fori_loop(0, groups, finish, 0)


def assimilate(send_index, obs_anom, innovation, obs_error, block_rows, taper_index, block_count,
               background):
    columns, places = block_rows.shape
    own, obs_count = obs_anom.shape
    values = background.shape[2]
    groups = columns // OGROUP
    bf16, f32 = jnp.bfloat16, jnp.float32
    dma = pltpu.SemaphoreType.DMA
    anywhere = pl.BlockSpec(memory_space=pl.ANY)
    return pl.pallas_call(
        kernel,
        out_shape=jax.ShapeDtypeStruct((MEMBERS, columns, own, values), bf16),
        in_specs=[anywhere] + [VMEM_SPEC] * 6 + [SMEM_SPEC, anywhere],
        out_specs=anywhere,
        scratch_shapes=[
            pltpu.SMEM((2, REGIONS, SLOT), jnp.int32),
            pltpu.VMEM((2, REGIONS, SLOT), jnp.int32),
            pltpu.VMEM((own, obs_count), bf16),
            pltpu.VMEM((2, MEMBERS, own, obs_count), bf16),
            pltpu.VMEM((own, obs_count), bf16),
            pltpu.VMEM((2, obs_count // LANES, LANES), bf16),
            pltpu.VMEM((2 * obs_count, K), f32),
            pltpu.VMEM((BLOCKS, K, SLOT), bf16),
            pltpu.VMEM((BLOCKS, 1, SLOT), f32),
            pltpu.VMEM((REGIONS, K, SLOT), bf16),
            pltpu.VMEM((REGIONS, 1, SLOT), f32),
            pltpu.VMEM((MEMBERS, own, columns, values), bf16),
            pltpu.VMEM((MEMBERS, columns, own, values), bf16),
            pltpu.VMEM((MEMBERS, columns, own, values), bf16),
            pltpu.VMEM((columns, LANES, LANES), f32),
            pltpu.VMEM((columns, places), f32),
            pltpu.VMEM((K + 16, 2 * SLOT), bf16),
            pltpu.VMEM((K + 16, columns * K), f32),
            dma((2,)),
            dma((2, MEMBERS)),
            dma((2, MEMBERS)),
            dma((2, MEMBERS)),
            dma((3,)),
            dma((3,)),
            dma((MEMBERS,)),
            dma((MEMBERS,)),
            dma((BLOCKS,)),
            dma((REGIONS,)),
            dma((BLOCKS,)),
            dma((REGIONS,)),
            dma((groups, MEMBERS)),
            dma((groups, MEMBERS)),
        ],
        compiler_params=pltpu.CompilerParams(
            vmem_limit_bytes=56 * 2**20, collective_id=0, has_side_effects=True
        ),
        cost_estimate=pl.CostEstimate(
            flops=2 * 10**10, bytes_accessed=12 * 2**20, transcendentals=0
        ),
    )(
        send_index,
        obs_anom,
        obs_error.reshape(1, obs_count),
        innovation.reshape(-1, LANES),
        obs_error.reshape(-1, LANES),
        block_rows,
        taper_index,
        block_count,
        background,
    )


def shards(
    background, obs_anom, innovation, obs_error, send_index, block_index, block_count, taper_index
):
    result = assimilate(
        send_index, obs_anom, innovation, obs_error, block_index[0, 0], taper_index[0, 0],
        block_count[0, 0], background,
    )
    return restore(result)


def solution(mesh):
    in_specs = (
        P("member", "region", None),
        P("member", "region"),
        P("region"),
        P("region"),
        P("region", None, None, None),
        P("region", "member", None, None),
        P("region", "member", None),
        P("region", "member", None, None),
    )
    out_specs = P("member", "region", None)
    return jax.shard_map(shards, mesh=mesh, in_specs=in_specs, out_specs=out_specs, check_vma=False)
```

```python
import jax
import jax.numpy as jnp
from jax import lax
from jax.experimental import pallas as pl
from jax.experimental.pallas import tpu as pltpu
from jax.sharding import PartitionSpec as P

K = 128
SLOT = 512
NTAPER = 64
NS_ITERS = 6
LANES = 128
CGROUP = 4
OGROUP = 2
RESTORE_STEPS = 2
MEMBERS = 8
REGIONS = 32
NZ = 8
NY = 4
BLOCKS = 30
MESH = pl.DeviceIdType.MESH

NT = (((1,), (1,)), ((), ()))
VMEM_SPEC = pl.BlockSpec(memory_space=pltpu.VMEM)
SMEM_SPEC = pl.BlockSpec(memory_space=pltpu.SMEM)


def taper_weights(taper_index, block_count):
    radius = 2.0 * (taper_index.astype(jnp.float32) + 0.5) / NTAPER
    r2 = radius * radius
    r3 = r2 * radius
    r4 = r2 * r2
    r5 = r4 * radius
    inside_part = 1.0 - 5.0 / 3.0 * r2 + 0.625 * r3 + 0.5 * r4 - 0.25 * r5
    outside_part = (
        4.0 - 5.0 * radius + 5.0 / 3.0 * r2 + 0.625 * r3 - 0.5 * r4 + r5 / 12.0
        - 2.0 / (3.0 * radius)
    )
    weight = jnp.maximum(jnp.where(radius < 1.0, inside_part, outside_part), 0.0)
    places = lax.broadcasted_iota(jnp.int32, taper_index.shape, 1)
    return jnp.where(places < block_count, weight, 0.0)


def dev_pick(idx, dscaled):
    low = lax.broadcasted_iota(jnp.int32, (LANES, SLOT), 0) == (idx & (LANES - 1))
    picked = jnp.dot(
        dscaled, low.astype(jnp.float32).astype(jnp.bfloat16), preferred_element_type=jnp.float32
    )
    high = lax.broadcasted_iota(jnp.int32, picked.shape, 0) == (idx >> 7)
    return jnp.sum(jnp.where(high, picked, 0.0), axis=0, keepdims=True)


def split(x):
    high = x.astype(jnp.bfloat16)
    low = (x - high.astype(jnp.float32)).astype(jnp.bfloat16)
    return high, low


def dot3(a, b):
    ah, al = a
    bh, bl = b
    return jnp.dot(
        jnp.concatenate([ah, al, ah], axis=1),
        jnp.concatenate([bh, bh, bl], axis=0),
        preferred_element_type=jnp.float32,
    )


def scatter_weights(c, bidx_ref, rho, wmat):
    p = bidx_ref[pl.ds(c, 1), :]
    weight = rho[pl.ds(c, 1), :]
    count = p.shape[1]
    rows = lax.broadcasted_iota(jnp.int32, (LANES, count), 0)
    first = (rows == (p >> 7)).astype(jnp.float32).astype(jnp.bfloat16)
    high = weight.astype(jnp.bfloat16).astype(jnp.float32)
    hit = rows == (p & (LANES - 1))
    second = jnp.concatenate(
        [
            jnp.where(hit, high, 0.0).astype(jnp.bfloat16),
            jnp.where(hit, weight - high, 0.0).astype(jnp.bfloat16),
        ],
        axis=0,
    )
    both = lax.dot_general(first, second, NT, preferred_element_type=jnp.float32)
    wmat[c] = both[:, :LANES] + both[:, LANES:]


def gram_blocks(parts, wmat, right, acc):
    columns = wmat.shape[0]
    lead = SLOT // LANES
    first = lax.broadcasted_iota(jnp.int32, (16, SLOT), 0) == 0
    values = []
    for b, (r, block, dev) in enumerate(parts):
        lanes = slice(b * SLOT, (b + 1) * SLOT)
        right[0:K, lanes] = block
        right[K : K + 16, lanes] = jnp.where(first, dev, 0.0).astype(jnp.bfloat16)
        values.append(block.astype(jnp.float32))
    for c in range(columns):
        pieces = []
        for v, (r, block, dev) in zip(values, parts):
            for q in range(lead):
                w = wmat[c, pl.ds(r * lead + q, 1), :]
                pieces.append((v[:, q * LANES : (q + 1) * LANES] * w).astype(jnp.bfloat16))
        acc[:, c * K : (c + 1) * K] += lax.dot_general(
            right[...], jnp.concatenate(pieces, axis=1), NT, preferred_element_type=jnp.float32
        )


def eye():
    shape = (K, K)
    same = lax.broadcasted_iota(jnp.int32, shape, 0) == lax.broadcasted_iota(jnp.int32, shape, 1)
    return same.astype(jnp.float32)


def transforms(grams, shifts):
    identity = eye()
    members = float(K)
    mats = [g + (members - 1.0) * identity for g in grams]
    norms = [jnp.sqrt(jnp.sum(m * m, axis=(0, 1), keepdims=True)) for m in mats]
    ys = [m / n for m, n in zip(mats, norms)]
    zs = [1.5 * identity - 0.5 * y for y in ys]
    ys = [dot3(split(z), split(y)) for z, y in zip(zs, ys)]
    for sweep in range(1, NS_ITERS):
        sy = [split(y) for y in ys]
        sz = [split(z) for z in zs]
        sf = [split(1.5 * identity - 0.5 * dot3(z, y)) for z, y in zip(sz, sy)]
        if sweep == NS_ITERS - 1:
            zs = [dot3(f, z) for f, z in zip(sf, sz)]
        else:
            both = [
                dot3(f, tuple(jnp.concatenate([a, b], axis=1) for a, b in zip(y, z)))
                for f, y, z in zip(sf, sy, sz)
            ]
            ys = [b[:, :K] for b in both]
            zs = [b[:, K:] for b in both]
    sz = [split(z) for z in zs]
    half = [dot3(split(p), z) for z, p in zip(sz, shifts)]
    full = [dot3(split(h), z) for z, h in zip(sz, half)]
    out = []
    for z, f, n in zip(zs, full, norms):
        out.append(jnp.sqrt(members - 1.0) * z / jnp.sqrt(n) + f[0:1, :] / n)
    return out


def analyse(c, transform, bg_ref, out_ref):
    state = bg_ref[:, c].reshape(K, bg_ref.shape[3]).astype(jnp.float32)
    mean_state = jnp.sum(state, axis=0, keepdims=True) * (1.0 / K)
    anomalies = (state - mean_state).astype(jnp.bfloat16)
    combined = jnp.dot(
        transform.astype(jnp.bfloat16), anomalies, preferred_element_type=jnp.float32
    )
    result = (mean_state + combined).astype(jnp.bfloat16)
    out_ref[:, c] = result.reshape(out_ref.shape[0], out_ref.shape[2], out_ref.shape[3])


def place(j):
    block = j + 2 * (j // 24)
    combo, dy = 2 * (block // 8) + block % 2, (block // 2) % 4
    distance = 2 - (combo + 2) // 4
    dz = distance * (1 - 2 * (combo % 2))
    slot = combo // 4 - combo // 7
    return slot, dz, dy


def region_at(z, y):
    return ((z + 16) % NZ) * NY + (y + 8) % NY


def swap_matrix(count):
    a = lax.broadcasted_iota(jnp.int32, (count, count), 0)
    b = lax.broadcasted_iota(jnp.int32, (count, count), 1)
    swap = (a // 16 == b % 16) & (a % 16 == b // 16)
    return swap.astype(jnp.float32).astype(jnp.bfloat16)


def swap_block(swap, block):
    rows = block.reshape(swap.shape[0], block.shape[2])
    moved = jnp.dot(swap, rows, preferred_element_type=jnp.float32).astype(jnp.bfloat16)
    return moved.reshape(block.shape)


def permute_state(raw, state):
    swap = swap_matrix(raw.shape[1] * raw.shape[2])
    for m in range(raw.shape[0]):
        state[m] = swap_block(swap, raw[m])


def restore_kernel(blocks_ref, out_ref):
    columns, own = blocks_ref.shape[1:3]
    swap = swap_matrix(columns * own)
    for m in range(blocks_ref.shape[0]):
        out_ref[:, m * columns : (m + 1) * columns, :] = swap_block(swap, blocks_ref[m])


def restore(blocks):
    members, columns, own, values = blocks.shape
    step = members // RESTORE_STEPS
    return pl.pallas_call(
        restore_kernel,
        grid=(RESTORE_STEPS,),
        out_shape=jax.ShapeDtypeStruct((own, members * columns, values), blocks.dtype),
        in_specs=[pl.BlockSpec((step, columns, own, values), lambda i: (i, 0, 0, 0))],
        out_specs=pl.BlockSpec((own, step * columns, values), lambda i: (0, i, 0)),
        compiler_params=pltpu.CompilerParams(vmem_limit_bytes=60 * 2**20),
    )(blocks)


def kernel(send_ref, obs_ref, err_ref, innov2_ref, err2_ref, bidx_ref, taper_ref,
           count_ref, bg_ref, out_ref,
           idx_smem, idx_ref, own, full, pair, dev2, table, sent, sent_dev, pool, pool_dev,
           raw, state, result, wmat, rho, right, acc,
           idx_sem, obs_send, obs_recv, forward_send, pair_send, pair_recv, bg_send, bg_recv,
           pool_send, pool_recv, dev_send, dev_recv, out_send, out_recv):
    me = lax.axis_index("member")
    region = lax.axis_index("region")
    z, y = region // NY, region % NY
    partner = region_at(z + 4, y)
    columns = bidx_ref.shape[0]
    obs_count = obs_ref.shape[1]
    others = [lax.rem(me + k, MEMBERS) for k in range(1, MEMBERS)]
    along = [lax.rem(me + k, MEMBERS) for k in range(2, MEMBERS, 2)]
    beside = me + 1 - 2 * lax.rem(me, 2)
    crossed = [lax.rem(beside + k, MEMBERS) for k in range(0, MEMBERS, 2)]

    own_idx = pltpu.make_async_copy(send_ref.at[0, me], idx_ref.at[0], idx_sem.at[0])
    own_idx.start()
    own_smem = pltpu.make_async_copy(send_ref.at[0, me], idx_smem.at[0], idx_sem.at[1])
    own_smem.start()
    barrier = pltpu.get_barrier_semaphore()
    for other in others:
        pl.semaphore_signal(barrier, inc=1, device_id={"member": other}, device_id_type=MESH)
    pl.semaphore_signal(barrier, inc=1, device_id={"region": partner}, device_id_type=MESH)
    near = [(dz, dy) for dz in (-2, -1, 0, 1, 2) for dy in range(NY) if (dz, dy) != (0, 0)]
    for dz, dy in near:
        pl.semaphore_signal(
            barrier, inc=1, device_id={"region": region_at(z + dz, y + dy)}, device_id_type=MESH
        )
    own[...] = (obs_ref[...].astype(jnp.float32) / err_ref[...]).astype(jnp.bfloat16)
    dev2[0] = (innov2_ref[...] / err2_ref[...]).astype(jnp.bfloat16)
    pl.semaphore_wait(barrier, len(others) + 1 + len(near))

    def remote(src, dst, send, recv, where):
        return pltpu.make_async_remote_copy(
            src_ref=src, dst_ref=dst, send_sem=send, recv_sem=recv,
            device_id=where, device_id_type=MESH,
        )

    def pair_copy():
        return remote(own, pair, pair_send.at[0], pair_recv.at[0], {"region": partner})

    def pair_dev_copy():
        return remote(dev2.at[0], dev2.at[1], pair_send.at[1], pair_recv.at[1],
                      {"region": partner})

    def pair_idx_copy():
        return remote(send_ref.at[0, me], idx_ref.at[1], pair_send.at[2], pair_recv.at[2],
                      {"region": partner})

    def forward_copy(slot, owner):
        return remote(full.at[slot, owner], full.at[slot, owner], forward_send.at[slot, owner],
                      obs_recv.at[slot, owner], {"member": beside})

    def obs_copy(src, slot, owner, to):
        return remote(src, full.at[slot, owner], obs_send.at[slot, to], obs_recv.at[slot, owner],
                      {"member": to})

    def bg_copy(owner, to):
        cols = pl.ds(pl.multiple_of(to * columns, columns), columns)
        return remote(bg_ref.at[:, cols, :], raw.at[owner], bg_send.at[to], bg_recv.at[owner],
                      {"member": to})

    def block_copy(j, source, to):
        return remote(sent.at[j], pool.at[source], pool_send.at[j], pool_recv.at[source],
                      {"region": to})

    def block_dev_copy(j, source, to):
        return remote(sent_dev.at[j], pool_dev.at[source], dev_send.at[j], dev_recv.at[source],
                      {"region": to})

    def out_copy(g, owner, to):
        cols = pl.ds(g * OGROUP, OGROUP)
        return remote(result.at[to, cols], out_ref.at[owner, cols], out_send.at[g, to],
                      out_recv.at[g, owner], {"member": to})

    def spread(src, slot):
        for other in along + [beside]:
            obs_copy(src, slot, me, other).start()
        full[slot, me] = src[...]

    def forward(slot):
        for other in along:
            obs_copy(own, slot, other, other).wait_recv()
            forward_copy(slot, other).start()

    pair_copy().start()
    pair_dev_copy().start()
    pair_idx_copy().start()
    spread(own, 0)

    for c in range(columns):
        rho[pl.ds(c, 1), :] = taper_weights(taper_ref[pl.ds(c, 1), :], count_ref[c])

    def scatter(i, _):
        scatter_weights(2 * i, bidx_ref, rho, wmat)
        scatter_weights(2 * i + 1, bidx_ref, rho, wmat)
        return 0

    lax.fori_loop(0, columns // 2, scatter, 0)
    acc[...] = jnp.zeros_like(acc)

    forward(0)
    pair_copy().wait_recv()
    spread(pair, 1)
    own_idx.wait()
    own_smem.wait()

    def build(slot):
        for other in crossed:
            obs_copy(own, slot, other, other).wait_recv()
        for q in range(obs_count // SLOT):
            part = full[slot, :, :, q * SLOT : (q + 1) * SLOT]
            part = part.reshape(K, SLOT).astype(jnp.float32)
            table[pl.ds(slot * obs_count + q * SLOT, SLOT), :] = part.T

    def gather(slot, to):
        start = slot * obs_count
        parts = []
        for h in range(SLOT // LANES):
            rows = [
                table[pl.ds(idx_smem[slot, to, h * LANES + j] + start, 1), :] for j in range(LANES)
            ]
            parts.append(jnp.concatenate(rows, axis=0).T.astype(jnp.bfloat16))
        picked = dev_pick(idx_ref[slot, pl.ds(to, 1), :], dev2[slot])
        return jnp.concatenate(parts, axis=1), picked

    def send(j, _):
        slot, dz, dy = place(j)
        to = region_at(z + dz, y + dy)
        source = region_at(z + 4 * slot, y)
        block, dev = gather(slot, to)
        sent[j] = block
        sent_dev[j] = dev
        block_copy(j, source, to).start()
        block_dev_copy(j, source, to).start()
        return 0

    build(0)
    lax.fori_loop(0, 10, send, 0)
    forward(1)
    lax.fori_loop(10, 16, send, 0)
    pair_dev_copy().wait_recv()
    pair_idx_copy().wait_recv()
    pair_smem = pltpu.make_async_copy(idx_ref.at[1], idx_smem.at[1], idx_sem.at[0])
    pair_smem.start()
    for other in others:
        bg_copy(me, other).start()
    own_cols = pl.ds(pl.multiple_of(me * columns, columns), columns)
    keep_bg = pltpu.make_async_copy(bg_ref.at[:, own_cols, :], raw.at[me], bg_send.at[me])
    keep_bg.start()
    build(1)
    pair_smem.wait()
    lax.fori_loop(16, BLOCKS, send, 0)

    def local(slot, _):
        source = region_at(z + 4 * slot, y)
        block, dev = gather(slot, region)
        pool[source] = block
        pool_dev[source] = dev
        return 0

    lax.fori_loop(0, 2, local, 0)

    def add(sources):
        parts = [(source, pool[source], pool_dev[source]) for source in sources]
        gram_blocks(parts, wmat, right, acc)

    add([region, partner])

    def receive(i, _):
        sources = []
        for j in (2 * i, 2 * i + 1):
            slot, dz, dy = place(j)
            source = region_at(z - dz + 4 * slot, y - dy)
            block_copy(j, source, region).wait_recv()
            block_dev_copy(j, source, region).wait_recv()
            sources.append(source)
        add(sources)
        return 0

    lax.fori_loop(0, 8, receive, 0)
    keep_bg.wait()
    for other in others:
        bg_copy(other, other).wait_recv()
    permute_state(raw, state)
    lax.fori_loop(8, BLOCKS // 2, receive, 0)

    def own_out(g):
        cols = pl.ds(g * OGROUP, OGROUP)
        return pltpu.make_async_copy(result.at[me, cols], out_ref.at[me, cols], out_send.at[g, me])

    def group(i, _):
        first = i * CGROUP
        where = [pl.ds(pl.multiple_of((first + k) * K, K), K) for k in range(CGROUP)]
        grams = [acc[0:K, w] for w in where]
        shifts = [acc[K : K + 16, w] for w in where]
        done = transforms(grams, shifts)
        for h in range(CGROUP // OGROUP):
            g = i * (CGROUP // OGROUP) + h
            for k in range(OGROUP):
                at = h * OGROUP + k
                analyse(first + at, done[at], state, result)
            for other in others:
                out_copy(g, me, other).start()
            own_out(g).start()
        return 0

    groups = columns // OGROUP
    lax.fori_loop(0, columns // CGROUP, group, 0)

    pair_copy().wait_send()
    pair_dev_copy().wait_send()
    pair_idx_copy().wait_send()
    for other in along + [beside]:
        obs_copy(own, 0, me, other).wait_send()
        obs_copy(pair, 1, me, other).wait_send()
    for other in along:
        forward_copy(0, other).wait_send()
        forward_copy(1, other).wait_send()
    for other in others:
        bg_copy(me, other).wait_send()

    def drain(j, _):
        block_copy(j, region, region).wait_send()
        block_dev_copy(j, region, region).wait_send()
        return 0

    lax.fori_loop(0, BLOCKS, drain, 0)

    def finish(g, _):
        for other in others:
            out_copy(g, me, other).wait_send()
            out_copy(g, other, other).wait_recv()
        own_out(g).wait()
        return 0

    lax.fori_loop(0, groups, finish, 0)


def assimilate(send_index, obs_anom, innovation, obs_error, block_rows, taper_index, block_count,
               background):
    columns, places = block_rows.shape
    own, obs_count = obs_anom.shape
    values = background.shape[2]
    groups = columns // OGROUP
    bf16, f32 = jnp.bfloat16, jnp.float32
    dma = pltpu.SemaphoreType.DMA
    anywhere = pl.BlockSpec(memory_space=pl.ANY)
    return pl.pallas_call(
        kernel,
        out_shape=jax.ShapeDtypeStruct((MEMBERS, columns, own, values), bf16),
        in_specs=[anywhere] + [VMEM_SPEC] * 6 + [SMEM_SPEC, anywhere],
        out_specs=anywhere,
        scratch_shapes=[
            pltpu.SMEM((2, REGIONS, SLOT), jnp.int32),
            pltpu.VMEM((2, REGIONS, SLOT), jnp.int32),
            pltpu.VMEM((own, obs_count), bf16),
            pltpu.VMEM((2, MEMBERS, own, obs_count), bf16),
            pltpu.VMEM((own, obs_count), bf16),
            pltpu.VMEM((2, obs_count // LANES, LANES), bf16),
            pltpu.VMEM((2 * obs_count, K), f32),
            pltpu.VMEM((BLOCKS, K, SLOT), bf16),
            pltpu.VMEM((BLOCKS, 1, SLOT), f32),
            pltpu.VMEM((REGIONS, K, SLOT), bf16),
            pltpu.VMEM((REGIONS, 1, SLOT), f32),
            pltpu.VMEM((MEMBERS, own, columns, values), bf16),
            pltpu.VMEM((MEMBERS, columns, own, values), bf16),
            pltpu.VMEM((MEMBERS, columns, own, values), bf16),
            pltpu.VMEM((columns, LANES, LANES), f32),
            pltpu.VMEM((columns, places), f32),
            pltpu.VMEM((K + 16, 2 * SLOT), bf16),
            pltpu.VMEM((K + 16, columns * K), f32),
            dma((2,)),
            dma((2, MEMBERS)),
            dma((2, MEMBERS)),
            dma((2, MEMBERS)),
            dma((3,)),
            dma((3,)),
            dma((MEMBERS,)),
            dma((MEMBERS,)),
            dma((BLOCKS,)),
            dma((REGIONS,)),
            dma((BLOCKS,)),
            dma((REGIONS,)),
            dma((groups, MEMBERS)),
            dma((groups, MEMBERS)),
        ],
        compiler_params=pltpu.CompilerParams(
            vmem_limit_bytes=56 * 2**20, collective_id=0, has_side_effects=True
        ),
        cost_estimate=pl.CostEstimate(
            flops=2 * 10**10, bytes_accessed=12 * 2**20, transcendentals=0
        ),
    )(
        send_index,
        obs_anom,
        obs_error.reshape(1, obs_count),
        innovation.reshape(-1, LANES),
        obs_error.reshape(-1, LANES),
        block_rows,
        taper_index,
        block_count,
        background,
    )


def shards(
    background, obs_anom, innovation, obs_error, send_index, block_index, block_count, taper_index
):
    result = assimilate(
        send_index, obs_anom, innovation, obs_error, block_index[0, 0], taper_index[0, 0],
        block_count[0, 0], background,
    )
    return restore(result)


def solution(mesh):
    in_specs = (
        P("member", "region", None),
        P("member", "region"),
        P("region"),
        P("region"),
        P("region", None, None, None),
        P("region", "member", None, None),
        P("region", "member", None),
        P("region", "member", None, None),
    )
    out_specs = P("member", "region", None)
    return jax.shard_map(shards, mesh=mesh, in_specs=in_specs, out_specs=out_specs, check_vma=False)
```
